256 devices in a mesh: batch: 8 (over y_hi, x), tile: 32 (over z, y_lo, core).
Axes of the slice: x: 4, y: 4 (y_hi: 2, y_lo: 2; y = y_hi * 2 + y_lo), z: 8, core: 2. Of those that a mesh axis runs over, the one named last changes fastest.
Arguments:
- queries: bfloat16 [8, 4096, 2048], P('batch', 'tile'), may hold values from -120 to 120
- keys: bfloat16 [8, 4096, 2048], P('batch', 'tile'), may hold values from -6 to 6
- values: bfloat16 [8, 4096, 2048], P('batch', 'tile'), may hold values from -6 to 6
- grad_out: bfloat16 [8, 4096, 2048], P('batch', 'tile'), may hold values from -6 to 6
- valid: int32 [8, 4096], P('batch'), may hold values from 0 to 1, as said below
- scale_ids: int32 [4096], replicated, may hold values from 0 to 12, as said below
- scale_bias: float32 [16, 13, 13], replicated, may hold values from -6 to 6
Outputs:
- attended: bfloat16 [8, 4096, 2048], P('batch', 'tile')
- grad_queries: bfloat16 [8, 4096, 2048], P('batch', 'tile')
- grad_keys: bfloat16 [8, 4096, 2048], P('batch', 'tile')
- grad_values: bfloat16 [8, 4096, 2048], P('batch', 'tile')
- grad_bias: float32 [16, 13, 13], replicated
The draws below stay inside these ranges and needn't reach their ends.
Inputs may be any that keep to these rules, and one draw needn't show every extreme that they name: Coarse tokens are always valid; in each tile the valid fine tokens form a leading run of 30 to 120 tokens, and in every image some tile has all its fine tokens valid. `scale_ids`: over the coarse tokens taken tile by tile in order, scale ids never fall, start at 0 and end at 8; within each tile the fine tokens carry scales 9 to 12, never falling, the first one 9 and the last 12.
All inputs are finite; a program needn't handle non-finite values.
Results may differ from the reference program's by a relative error of at most 0.0059.
Values may be sent and summed in bfloat16 or wider, within the bound.
No kernel may reach another device: no remote copies, remote signals or barrier semaphores. Data moves between devices by JAX's collectives and lax.ppermute only.
A program may use at most 128 MiB of HBM per device.

```python
import math
import jax
import jax.numpy as jnp
from jax import lax

HEADS = 16
DH = 128
LEVELS = 13
C_DEV = 8
F_DEV = 120
HD = 2048
ROWS_DEV = 128
TOKENS = 4096
IMGS = 8


def shared_keys(key):
    return jnp.clip(jax.random.normal(key, (IMGS, TOKENS, HD), jnp.float32), -6.0, 6.0)


def draw_keys(key, part):
    return shared_keys(key).astype(jnp.bfloat16)


def draw_queries(key, part):
    key = jax.random.fold_in(key, 3)
    fresh_draw = jnp.clip(jax.random.normal(key, (IMGS, TOKENS, HD), jnp.float32), -6.0, 6.0)
    return fresh_draw.astype(jnp.bfloat16)


def draw_valid(key, part):
    key = jax.random.fold_in(key, 5)
    tile_count = TOKENS // ROWS_DEV
    cut_rows = jax.random.randint(key, (IMGS, tile_count), F_DEV // 4, F_DEV + 1)
    full_key = jax.random.fold_in(key, 7)
    full_tile = jax.random.randint(full_key, (IMGS,), 0, tile_count)
    tile_ids = jnp.arange(tile_count, dtype=jnp.int32)
    cut_rows = jnp.where(tile_ids[None, :] == full_tile[:, None], F_DEV, cut_rows)
    inner_pos = jnp.arange(ROWS_DEV, dtype=jnp.int32)
    valid_mask = (inner_pos[None, None, :] < C_DEV) | ((inner_pos - C_DEV)[None, None, :] < cut_rows[:, :, None])
    return valid_mask.astype(jnp.int32).reshape(IMGS, TOKENS)


def draw_scale_ids(key, part):
    key = jax.random.fold_in(key, 9)
    tile_count = TOKENS // ROWS_DEV
    coarse_total = tile_count * C_DEV
    bounds = jax.random.randint(key, (LEVELS - 5,), 1, max(coarse_total, 2))
    coarse_pos = jnp.arange(coarse_total, dtype=jnp.int32)
    coarse_ids = jnp.sum((coarse_pos[:, None] >= bounds[None, :]).astype(jnp.int32), axis=1)
    fine_key = jax.random.fold_in(key, 11)
    fine_bounds = jax.random.randint(fine_key, (tile_count, 3), 1, F_DEV)
    fine_pos = jnp.arange(F_DEV, dtype=jnp.int32)
    fine_ids = LEVELS - 4 + jnp.sum((fine_pos[None, :, None] >= fine_bounds[:, None, :]).astype(jnp.int32), axis=2)
    scale_grid = jnp.concatenate([coarse_ids.reshape(tile_count, C_DEV), fine_ids], axis=1)
    return scale_grid.reshape(TOKENS).astype(jnp.int32)


def block_levels(own_key, dims, shards, low, high):
    loudness = 1.0
    for dim, parts in shards:
        heights = jax.random.uniform(jax.random.fold_in(jax.random.fold_in(own_key, 6), dim), (parts,), jnp.float32, low / len(shards), high / len(shards))
        loudness = loudness * jnp.repeat(jnp.exp(heights), dims[dim] // parts).reshape((-1,) + (1,) * (len(dims) - 1 - dim))
    return loudness


def centred(own_key, dims, spread, most, cuts=(), held_as=jnp.bfloat16):
    loudness = block_levels(own_key, dims, cuts, -0.22, 0.18) if cuts else 1.0
    drawn = jax.random.normal(own_key, dims, jnp.float32) * spread * loudness
    return jnp.minimum(jnp.maximum(drawn, -most), most).astype(held_as)


def setup_inputs(seed: int = 0) -> dict:
    arg_keys = jax.random.split(jax.random.key(seed), 8)
    return {
        "queries": draw_queries(jax.random.fold_in(arg_keys[7], 71), 0),
        "keys": draw_keys(jax.random.fold_in(arg_keys[7], 71), 0),
        "values": centred(arg_keys[2], (IMGS, TOKENS, HD), 1.0, 6.0, ((0, 8), (1, 32))),
        "grad_out": centred(arg_keys[3], (IMGS, TOKENS, HD), 1.0, 6.0, ((0, 8), (1, 32))),
        "valid": draw_valid(jax.random.fold_in(arg_keys[7], 71), 0),
        "scale_ids": draw_scale_ids(jax.random.fold_in(arg_keys[7], 71), 0),
        "scale_bias": centred(arg_keys[6], (HEADS, LEVELS, LEVELS), 1.0, 6.0, (), jnp.float32),
    }


masked_value = -1e+30

def reference(queries, keys, values, grad_out, valid, scale_ids, scale_bias):
    row_count = C_DEV + F_DEV
    tile_count = TOKENS // row_count
    inv_scale = 1.0 / math.sqrt(DH)
    scale_grid = scale_ids.reshape(tile_count, row_count)
    coarse_scale = scale_grid[:, :C_DEV].reshape(-1)
    padded_scale = jnp.pad(scale_grid[:, C_DEV:], ((1, 1), (0, 0)))
    level_ids = jnp.arange(LEVELS, dtype=jnp.int32)
    coarse_total = tile_count * C_DEV
    highest = lax.Precision.HIGHEST

    def one_image(inputs):
        image_q, image_k, image_v, image_g, image_valid = inputs
        shaped_q = image_q.reshape(tile_count, row_count, HEADS, DH)
        shaped_k = image_k.reshape(tile_count, row_count, HEADS, DH)
        shaped_v = image_v.reshape(tile_count, row_count, HEADS, DH)
        shaped_g = image_g.reshape(tile_count, row_count, HEADS, DH)
        valid_grid = image_valid.reshape(tile_count, row_count)
        coarse_k = shaped_k[:, :C_DEV].reshape(coarse_total, HEADS, DH)
        coarse_v = shaped_v[:, :C_DEV].reshape(coarse_total, HEADS, DH)
        coarse_valid = valid_grid[:, :C_DEV].reshape(-1)
        padded_k = jnp.pad(shaped_k[:, C_DEV:], ((1, 1), (0, 0), (0, 0), (0, 0)))
        padded_v = jnp.pad(shaped_v[:, C_DEV:], ((1, 1), (0, 0), (0, 0), (0, 0)))
        padded_valid = jnp.pad(valid_grid[:, C_DEV:], ((1, 1), (0, 0)))

        def tile_step(state_carry, tile_now):
            grad_ck, grad_cv, grad_pk, grad_pv, grad_sb = state_carry
            query_tile = lax.dynamic_index_in_dim(shaped_q, tile_now, 0, keepdims=False)
            upstream = lax.dynamic_index_in_dim(shaped_g, tile_now, 0, keepdims=False)
            own_scale = lax.dynamic_index_in_dim(scale_grid, tile_now, 0, keepdims=False)
            own_valid = lax.dynamic_index_in_dim(valid_grid, tile_now, 0, keepdims=False)
            near_k = lax.dynamic_slice_in_dim(padded_k, tile_now, 3, 0).reshape(3 * F_DEV, HEADS, DH)
            near_v = lax.dynamic_slice_in_dim(padded_v, tile_now, 3, 0).reshape(3 * F_DEV, HEADS, DH)
            key_all = jnp.concatenate([coarse_k, near_k], axis=0).astype(jnp.float32)
            value_all = jnp.concatenate([coarse_v, near_v], axis=0).astype(jnp.float32)
            key_scale = jnp.concatenate([coarse_scale, lax.dynamic_slice_in_dim(padded_scale, tile_now, 3, 0).reshape(-1)])
            key_valid = jnp.concatenate([coarse_valid, lax.dynamic_slice_in_dim(padded_valid, tile_now, 3, 0).reshape(-1)])
            admitted = (key_scale[None, :] <= own_scale[:, None]) & (key_valid[None, :] > 0)
            query_f = query_tile.astype(jnp.float32)
            scores = jnp.einsum('rhd,khd->hrk', query_f, key_all) * inv_scale + scale_bias[:, own_scale[:, None], key_scale[None, :]]
            scores = jnp.where(admitted[None], scores, masked_value)
            row_peak = lax.optimization_barrier(jnp.max(scores, axis=-1, keepdims=True))
            exponent = jnp.exp(scores - row_peak)
            probs = exponent / lax.optimization_barrier(jnp.sum(exponent, axis=-1, keepdims=True))
            probs_b = lax.optimization_barrier(probs.astype(jnp.bfloat16)).astype(jnp.float32)
            mixed = jnp.einsum('hrk,khd->rhd', probs_b, value_all)
            keep_row = (own_valid > 0)[:, None, None]
            attended = jnp.where(keep_row, mixed, 0.0).astype(jnp.bfloat16)
            grad_in = jnp.where(keep_row, upstream, jnp.zeros_like(upstream)).astype(jnp.float32)
            grad_probs = jnp.einsum('rhd,khd->hrk', grad_in, value_all)
            delta_row = lax.optimization_barrier(jnp.sum(grad_in * mixed, axis=-1)).T
            grad_scores = probs * (grad_probs - delta_row[:, :, None])
            onehot_rows = (own_scale[:, None] == level_ids[None, :]).astype(jnp.float32)
            onehot_cols = (key_scale[:, None] == level_ids[None, :]).astype(jnp.float32)
            by_level = jnp.einsum('hrk,kb->hrb', grad_scores, onehot_cols, precision=highest)
            grad_sb = grad_sb + jnp.einsum('rs,hrb->hsb', onehot_rows, by_level, precision=highest)
            scores_b = lax.optimization_barrier(grad_scores.astype(jnp.bfloat16)).astype(jnp.float32)
            grad_q = (jnp.einsum('hrk,khd->rhd', scores_b, key_all) * inv_scale).astype(jnp.bfloat16)
            grad_k = jnp.einsum('hrk,rhd->khd', scores_b, query_f) * inv_scale
            grad_v = jnp.einsum('hrk,rhd->khd', probs_b, grad_in)
            grad_ck = grad_ck + grad_k[:coarse_total]
            grad_cv = grad_cv + grad_v[:coarse_total]
            window_k = lax.dynamic_slice_in_dim(grad_pk, tile_now, 3, 0) + grad_k[coarse_total:].reshape(3, F_DEV, HEADS, DH)
            window_v = lax.dynamic_slice_in_dim(grad_pv, tile_now, 3, 0) + grad_v[coarse_total:].reshape(3, F_DEV, HEADS, DH)
            grad_pk = lax.dynamic_update_slice_in_dim(grad_pk, window_k, tile_now, 0)
            grad_pv = lax.dynamic_update_slice_in_dim(grad_pv, window_v, tile_now, 0)
            return ((grad_ck, grad_cv, grad_pk, grad_pv, grad_sb), (attended, grad_q))
        start_state = (jnp.zeros((coarse_total, HEADS, DH), jnp.float32), jnp.zeros((coarse_total, HEADS, DH), jnp.float32), jnp.zeros((tile_count + 2, F_DEV, HEADS, DH), jnp.float32), jnp.zeros((tile_count + 2, F_DEV, HEADS, DH), jnp.float32), jnp.zeros((HEADS, LEVELS, LEVELS), jnp.float32))
        final_state, stacked = lax.scan(tile_step, start_state, jnp.arange(tile_count, dtype=jnp.int32))
        grad_ck, grad_cv, grad_pk, grad_pv, grad_sb = final_state
        grad_keys = jnp.concatenate([grad_ck.reshape(tile_count, C_DEV, HEADS, DH), grad_pk[1:-1]], axis=1)
        grad_values = jnp.concatenate([grad_cv.reshape(tile_count, C_DEV, HEADS, DH), grad_pv[1:-1]], axis=1)
        return (stacked[0].reshape(TOKENS, HD), stacked[1].reshape(TOKENS, HD), grad_keys.reshape(TOKENS, HD).astype(jnp.bfloat16), grad_values.reshape(TOKENS, HD).astype(jnp.bfloat16), grad_sb)
    results = lax.map(one_image, (queries, keys, values, grad_out, valid))
    return (results[0], results[1], results[2], results[3], lax.optimization_barrier(jnp.sum(results[4], axis=0)))
```

```python
import functools
import math

import jax
import jax.numpy as jnp
from jax import lax
from jax.experimental import pallas as pl
from jax.experimental.pallas import tpu as pltpu
from jax.sharding import PartitionSpec as P

COARSE = 8
MASKED = -1e30
LANES = 128
SLOT = 16
BF16 = jnp.bfloat16
F32 = jnp.float32
OFFSETS = (0, 1, 2, 3, 4, -3, -2, -1)


def mm(a, b, contract):
    return lax.dot_general(a, b, (contract, ((), ())), preferred_element_type=F32)


ROW_COL = ((1,), (0,))
ROW_ROW = ((1,), (1,))
COL_COL = ((0,), (0,))


def attention_kernel(inv_scale, half_ref, *refs):
    (q_ref, k_ref, v_ref, g_ref, kv_par, qg_par, kv_own_out, kv_par_out) = refs[:8]
    coarse_refs = refs[8:16]
    row_hot_ref, key_hot_ref, table_ref, keep_ref = refs[16:20]
    own_ref, par_ref, own_out_ref, par_out_ref = refs[20:24]
    coarse_out = refs[24:32]
    bias_ref = refs[32]
    step = pl.program_id(0)
    rows = q_ref.shape[0]
    part = coarse_refs[0].shape[0] // 2
    total = part * len(coarse_refs)
    keep = keep_ref[...] > 0.0
    q = jnp.concatenate([q_ref[...], qg_par[:rows]], axis=0)
    g_all = jnp.concatenate([g_ref[...], qg_par[rows:]], axis=0)
    g = jnp.where(keep, g_all.astype(F32), 0.0).astype(BF16)
    row_hot = row_hot_ref[...]
    key_hot = key_hot_ref[...]
    k_main = jnp.concatenate([r[:part] for r in coarse_refs] + [k_ref[...], kv_par[:rows]], axis=0)
    v_main = jnp.concatenate([r[part:] for r in coarse_refs] + [v_ref[...], kv_par[rows:]], axis=0)
    main = k_main.shape[0]
    hot_main = key_hot[:main]
    hot_own = key_hot[main : main + rows]
    hot_par = key_hot[main + rows :]
    row_bias = mm(row_hot, table_ref[0], ROW_COL).astype(BF16)
    q_ext = jnp.concatenate([q, row_bias], axis=1)
    k_main_ext = jnp.concatenate([k_main, hot_main], axis=1)
    k_own_ext = jnp.concatenate([kv_own_out[:rows], hot_own], axis=1)
    k_par_ext = jnp.concatenate([kv_par_out[:rows], hot_par], axis=1)
    v_own = kv_own_out[rows:]
    v_par = kv_par_out[rows:]

    def stacked(a, own, par, contract):
        return jnp.concatenate([mm(a[:rows], own, contract), mm(a[rows:], par, contract)], axis=0)

    s_main = mm(q_ext, k_main_ext, ROW_ROW) * inv_scale
    s_out = stacked(q_ext, k_own_ext, k_par_ext, ROW_ROW) * inv_scale
    peak = jnp.maximum(
        jnp.max(s_main, axis=1, keepdims=True), jnp.max(s_out, axis=1, keepdims=True)
    )
    e_main = jnp.exp(s_main - peak)
    e_out = jnp.exp(s_out - peak)
    norm = 1.0 / (
        jnp.sum(e_main, axis=1, keepdims=True) + jnp.sum(e_out, axis=1, keepdims=True)
    )
    p_main = e_main * norm
    p_out = e_out * norm
    pb_main = p_main.astype(BF16)
    pb_out = p_out.astype(BF16)
    mixed = mm(pb_main, v_main, ROW_COL) + stacked(pb_out, v_own, v_par, ROW_COL)
    attended = jnp.where(keep, mixed, 0.0).astype(BF16)
    delta = jnp.sum(g.astype(F32) * mixed, axis=1, keepdims=True)
    d_main = p_main * (mm(g, v_main, ROW_ROW) - delta)
    d_out = p_out * (stacked(g, v_own, v_par, ROW_ROW) - delta)
    db_main = d_main.astype(BF16)
    db_out = d_out.astype(BF16)
    dl_main = (d_main - db_main.astype(F32)).astype(BF16)
    dl_out = (d_out - db_out.astype(F32)).astype(BF16)
    q_terms = mm(db_main, k_main_ext, ROW_COL) + stacked(db_out, k_own_ext, k_par_ext, ROW_COL)
    grad_q = (q_terms[:, :LANES] * inv_scale).astype(BF16)
    by_level = q_terms[:, LANES:] + (
        mm(dl_main, hot_main, ROW_COL) + stacked(dl_out, hot_own, hot_par, ROW_COL)
    )
    bias = lax.dot_general(
        row_hot.astype(F32),
        by_level,
        (COL_COL, ((), ())),
        precision=lax.Precision.HIGHEST,
        preferred_element_type=F32,
    )
    lane = lax.broadcasted_iota(jnp.int32, bias.shape, 1)
    bias = jnp.where(lane < SLOT, bias, 0.0)
    bias = pltpu.roll(bias, step * SLOT, 1)

    @pl.when(step == 0)
    def _():
        bias_ref[...] = bias

    @pl.when(step > 0)
    def _():
        bias_ref[...] = bias_ref[...] + bias

    gk_main = (mm(db_main, q, COL_COL) * inv_scale).astype(BF16)
    gv_main = mm(pb_main, g, COL_COL).astype(BF16)
    gk_own = (mm(db_out[:rows], q[:rows], COL_COL) * inv_scale).astype(BF16)
    gk_par = (mm(db_out[rows:], q[rows:], COL_COL) * inv_scale).astype(BF16)
    gv_own = mm(pb_out[:rows], g[:rows], COL_COL).astype(BF16)
    gv_par = mm(pb_out[rows:], g[rows:], COL_COL).astype(BF16)
    for place, ref in ((0, own_ref), (1, par_ref)):
        here = slice(place * rows, (place + 1) * rows)
        there = slice(total + place * rows, total + (place + 1) * rows)
        ref[0 * rows : 1 * rows] = attended[here]
        ref[1 * rows : 2 * rows] = grad_q[here]
        ref[2 * rows : 3 * rows] = gk_main[there]
        ref[3 * rows : 4 * rows] = gv_main[there]
    own_out_ref[:rows] = gk_own
    own_out_ref[rows:] = gv_own
    par_out_ref[:rows] = gk_par
    par_out_ref[rows:] = gv_par
    for j, ref in enumerate(coarse_out):
        ref[:part] = gk_main[j * part : (j + 1) * part]
        ref[part:] = gv_main[j * part : (j + 1) * part]


def call_kernel(inv_scale, half, full, pairs, coarse, tables, heads):
    rows, width = full[0].shape
    half_width = width // 2
    steps = heads // 2
    part2 = coarse[0].shape[0]
    row_hot, key_hot, table, keep = tables

    def mine(h, half_ref):
        return (0, half_ref[0] * steps + h)

    def at(h, half_ref):
        return (0, h)

    def fixed(h, half_ref):
        return (0, 0)

    in_specs = (
        [pl.BlockSpec((rows, LANES), mine)] * 4
        + [pl.BlockSpec((2 * rows, LANES), at)] * 4
        + [pl.BlockSpec((part2, LANES), at)] * len(coarse)
        + [
            pl.BlockSpec(row_hot.shape, fixed),
            pl.BlockSpec(key_hot.shape, fixed),
            pl.BlockSpec((1, SLOT, LANES), lambda h, half_ref: (half_ref[0] * steps + h, 0, 0)),
            pl.BlockSpec(keep.shape, fixed),
        ]
    )
    out_rows = [4 * rows] * 2 + [2 * rows] * 2 + [part2] * len(coarse)
    out_shape = [jax.ShapeDtypeStruct((r, half_width), BF16) for r in out_rows]
    out_shape.append(jax.ShapeDtypeStruct((SLOT, LANES), F32))
    out_specs = [pl.BlockSpec((r, LANES), at) for r in out_rows]
    out_specs.append(pl.BlockSpec((SLOT, LANES), fixed))
    return pl.pallas_call(
        functools.partial(attention_kernel, inv_scale),
        grid_spec=pltpu.PrefetchScalarGridSpec(
            num_scalar_prefetch=1, grid=(steps,), in_specs=in_specs, out_specs=out_specs
        ),
        out_shape=out_shape,
        compiler_params=pltpu.CompilerParams(
            dimension_semantics=("arbitrary",), vmem_limit_bytes=48 * 1024 * 1024
        ),
        cost_estimate=pl.CostEstimate(
            flops=12 * 2 * rows * 640 * half_width,
            bytes_accessed=10 * 1024 * 1024,
            transcendentals=steps * 2 * rows * 640,
        ),
    )(half, *full, *pairs, *coarse, row_hot, key_hot, table, keep)


def shards(queries, keys, values, grad_out, valid, scale_ids, scale_bias):
    q, k, v, g = queries[0], keys[0], values[0], grad_out[0]
    rows, width = q.shape
    half_width = width // 2
    heads, levels = scale_bias.shape[:2]
    tiles = lax.axis_size("tile")
    depth = tiles // 4
    images = lax.axis_size("batch")
    tile = lax.axis_index("tile")
    core = tile % 2
    inv_scale = 1.0 / math.sqrt(width // heads)

    def send(x, target):
        return lax.ppermute(x, "tile", [(i, target(i)) for i in range(tiles)])

    def to_core(x):
        return send(x, lambda i: i ^ 1)

    def to_side(x):
        return send(x, lambda i: i ^ 2)

    def to_depth(x, distance):
        return send(x, lambda i: (i + 4 * distance) % tiles)

    edge = []
    jump = []
    for i in range(tiles):
        near = i + 1 if i % 2 else i - 1
        far = i + 2 if i % 2 else i - 2
        if 0 <= near < tiles:
            edge.append((i, near))
        if 0 <= far < tiles:
            jump.append((i, far))

    def cut(x, which):
        return lax.dynamic_slice_in_dim(x, which * half_width, half_width, 1)

    small = jnp.stack([k[:COARSE], v[:COARSE]])
    small_mine = lax.dynamic_slice_in_dim(small, core * half_width, half_width, 2)
    small_other = lax.dynamic_slice_in_dim(small, (1 - core) * half_width, half_width, 2)
    chip = jnp.concatenate([small_mine, to_core(small_other)], axis=1).reshape(-1, half_width)
    side = to_side(chip)
    group = jnp.concatenate(
        [x[a : a + 2 * COARSE] for a in (0, 2 * COARSE) for x in (chip, side)], axis=0
    )
    blocks = {0: group}
    for d in (1, -1, 2, -2):
        blocks[d] = to_depth(group, -d)
    blocks[3] = to_depth(blocks[2], -1)
    blocks[-3] = to_depth(blocks[-2], 1)
    blocks[4] = send(
        jnp.where(core == 0, blocks[2], blocks[-2]),
        lambda i: (i + (8 if i % 2 else -8)) % tiles,
    )
    coarse = [blocks[d] for d in OFFSETS]

    kv_other = jnp.concatenate([cut(k, 1 - core), cut(v, 1 - core)], axis=0)
    kv_mine = jnp.concatenate([cut(k, core), cut(v, core)], axis=0)
    qg_other = jnp.concatenate([cut(q, 1 - core), cut(g, 1 - core)], axis=0)
    kv_own_out = lax.ppermute(kv_other, "tile", edge)
    kv_par_out = lax.ppermute(kv_mine, "tile", jump)
    kv_par = to_core(kv_other)
    qg_par = to_core(qg_other)

    valid_grid = valid[0].reshape(tiles, rows)
    scale_grid = scale_ids.reshape(tiles, rows)
    level_grid = jnp.where(valid_grid > 0, scale_grid, levels)
    inner = jnp.arange(rows, dtype=jnp.int32)
    fine_grid = jnp.where(inner[None, :] >= COARSE, level_grid, levels)
    near_grid = jnp.pad(fine_grid, ((1, 1), (0, 0)), constant_values=levels)
    partner = tile ^ 1
    outward = 2 * core - 1

    def line(grid, index):
        return lax.dynamic_index_in_dim(grid, index, 0, keepdims=False)

    z_here = tile // 4
    spots = jnp.stack([((z_here + d) % depth) * 4 + (j ^ (tile % 4)) for d in OFFSETS for j in range(4)])
    pick = (spots[:, None] == jnp.arange(tiles, dtype=jnp.int32)[None, :]).astype(F32)
    coarse_level = jnp.dot(
        pick, level_grid[:, :COARSE].astype(F32), precision=lax.Precision.HIGHEST
    ).astype(jnp.int32)
    key_level = jnp.concatenate(
        [
            coarse_level.reshape(-1),
            line(near_grid, tile + 1),
            line(near_grid, partner + 1),
            line(near_grid, tile + 1 + outward),
            line(near_grid, partner + 1 - outward),
        ]
    )
    column = jnp.arange(LANES, dtype=jnp.int32)
    key_hot = (
        (key_level[:, None] == (column % SLOT)[None, :]) & (column < 3 * SLOT)[None, :]
    ).astype(BF16)
    row_level = jnp.concatenate([line(scale_grid, tile), line(scale_grid, partner)])
    row_hot = (row_level[:, None] == jnp.arange(SLOT, dtype=jnp.int32)[None, :]).astype(BF16)
    keep = jnp.concatenate([line(valid_grid, tile), line(valid_grid, partner)]).astype(F32)[:, None]

    level_ids = jnp.arange(levels, dtype=jnp.int32)
    scaled = jnp.where(
        (level_ids[None, :] <= level_ids[:, None])[None], scale_bias / inv_scale, MASKED
    )
    scaled = jnp.pad(
        scaled,
        ((0, 0), (0, SLOT - levels), (0, SLOT - levels)),
        constant_values=MASKED,
    )
    parts = []
    rest = scaled
    for _ in range(3):
        piece = lax.reduce_precision(rest, 8, 7)
        parts.append(piece)
        rest = rest - piece
    table = jnp.pad(
        jnp.concatenate(parts, axis=2), ((0, 0), (0, 0), (0, LANES - 3 * SLOT))
    ).astype(BF16)

    results = call_kernel(
        inv_scale,
        core.reshape(1),
        (q, k, v, g),
        (kv_par, qg_par, kv_own_out, kv_par_out),
        coarse,
        (row_hot, key_hot, table, keep),
        heads,
    )
    own, par, own_out, par_out = results[:4]
    terms = dict(zip(OFFSETS, results[4:12]))
    bias = results[12]

    from_below = to_depth(terms[3], 1)
    from_above = to_depth(terms[-3], -1)
    across = send(terms[4], lambda i: (i + (-8 if i % 2 else 8)) % tiles)
    one_up = to_depth(terms[1], 1)
    one_down = to_depth(terms[-1], -1)

    def wide(x):
        return x.astype(F32)

    zero = jnp.zeros((), F32)
    two_up = wide(terms[2]) + wide(from_below) + jnp.where(core == 0, wide(across), zero)
    two_down = wide(terms[-2]) + wide(from_above) + jnp.where(core == 1, wide(across), zero)
    two_up = to_depth(two_up.astype(BF16), 2)
    two_down = to_depth(two_down.astype(BF16), -2)
    summed = wide(terms[0]) + wide(one_up) + wide(one_down) + wide(two_up) + wide(two_down)
    summed = summed.reshape(2, 2, 2 * COARSE, half_width)
    coarse_chip = summed[:, 0] + wide(to_side(summed[:, 1].astype(BF16)))
    coarse_mine = coarse_chip[:, :COARSE]
    coarse_other = wide(to_core(coarse_chip[:, COARSE:].astype(BF16)))

    back_other = lax.ppermute(own_out, "tile", edge)
    back_mine = lax.ppermute(par_out, "tile", [(b, a) for a, b in jump])
    other = to_core(par)

    both = ("batch", "tile")

    def everywhere(x, target):
        pairs = []
        for b in range(images):
            for i in range(tiles):
                b2, i2 = target(b, i)
                pairs.append((b * tiles + i, b2 * tiles + i2))
        return lax.ppermute(x, both, pairs)

    for shifts in ((2, 4, 6), (1,)):
        got = []
        for s in shifts:
            got.append(to_depth(bias, s))
        if len(shifts) == 1:
            got = [send(bias, lambda i: i ^ 2)]
            got.append(send(bias, lambda i: (i + 4) % tiles if (i // 4) % 2 == 0 else i - 4))
            got.append(send(bias, lambda i: ((i + 4) if (i // 4) % 2 == 0 else (i - 4)) ^ 2))
        for x in got:
            bias = bias + x
    x_count = images // 2
    got = [
        everywhere(bias, lambda b, i, s=s: ((b // x_count) * x_count + (b + s) % x_count, i))
        for s in range(1, x_count)
    ]
    for x in got:
        bias = bias + x
    same = everywhere(bias, lambda b, i: ((b + x_count) % images, i))
    swap = everywhere(bias, lambda b, i: (b, i ^ 1))
    cross = everywhere(bias, lambda b, i: ((b + x_count) % images, i ^ 1))
    mine_bias = bias + same
    other_bias = swap + cross
    bias_halves = jnp.where(
        core == 0, jnp.stack([mine_bias, other_bias]), jnp.stack([other_bias, mine_bias])
    )
    grad_bias = (
        bias_halves.reshape(2, SLOT, heads // 2, SLOT)
        .transpose(0, 2, 1, 3)
        .reshape(heads, SLOT, SLOT)[:, :levels, :levels]
    )

    def joined(mine, other_half):
        return jnp.where(
            core == 0,
            jnp.concatenate([mine, other_half], axis=-1),
            jnp.concatenate([other_half, mine], axis=-1),
        )

    attended = joined(own[:rows], other[:rows])
    grad_q = joined(own[rows : 2 * rows], other[rows : 2 * rows])
    fine_mine = wide(own[2 * rows :]) + wide(back_mine)
    fine_other = wide(other[2 * rows :]) + wide(back_other)
    fine = joined(fine_mine, fine_other).reshape(2, rows, width)
    coarse_rows = joined(coarse_mine, coarse_other)
    grads = jnp.concatenate([coarse_rows, fine[:, COARSE:]], axis=1).astype(BF16)
    return (attended[None], grad_q[None], grads[0][None], grads[1][None], grad_bias)


def solution(mesh):
    block = P("batch", "tile", None)
    return jax.shard_map(
        shards,
        mesh=mesh,
        in_specs=(block, block, block, block, P("batch", None), P(), P()),
        out_specs=(block, block, block, block, P()),
        check_vma=False,
    )
```

```python
import functools
import math

import jax
import jax.numpy as jnp
from jax import lax
from jax.experimental import pallas as pl
from jax.experimental.pallas import tpu as pltpu
from jax.sharding import PartitionSpec as P

COARSE = 8
MASKED = -1e30
LANES = 128
SLOT = 16
BF16 = jnp.bfloat16
F32 = jnp.float32
OFFSETS = (0, 2, -2, 4, 1, 3, -1, -3)


def after(x, *done):
    return lax.optimization_barrier((x, *done))[0]


def mm(a, b, contract):
    return lax.dot_general(a, b, (contract, ((), ())), preferred_element_type=F32)


ROW_COL = ((1,), (0,))
ROW_ROW = ((1,), (1,))
COL_COL = ((0,), (0,))


def attention_kernel(inv_scale, half_ref, *refs):
    (q_ref, k_ref, v_ref, g_ref, kv_par, qg_par, kv_own_out, kv_par_out) = refs[:8]
    coarse_refs = refs[8:14]
    row_hot_ref, key_hot_ref, table_ref, keep_ref = refs[14:18]
    own_ref, par_ref, own_out_ref, par_out_ref = refs[18:22]
    coarse_out = refs[22:28]
    bias_ref = refs[28]
    step = pl.program_id(0)
    rows = q_ref.shape[0]
    part = coarse_refs[0].shape[0] // 2
    places = [(r, a) for r in range(len(coarse_refs)) for a in range(0, coarse_refs[r].shape[0], 2 * part)]
    total = part * len(places)
    keep = keep_ref[...] > 0.0
    q = jnp.concatenate([q_ref[...], qg_par[:rows]], axis=0)
    g_all = jnp.concatenate([g_ref[...], qg_par[rows:]], axis=0)
    g = jnp.where(keep, g_all.astype(F32), 0.0).astype(BF16)
    row_hot = row_hot_ref[...]
    key_hot = key_hot_ref[...]
    k_main = jnp.concatenate([coarse_refs[r][a : a + part] for r, a in places] + [k_ref[...], kv_par[:rows]], axis=0)
    v_main = jnp.concatenate([coarse_refs[r][a + part : a + 2 * part] for r, a in places] + [v_ref[...], kv_par[rows:]], axis=0)
    main = k_main.shape[0]
    hot_main = key_hot[:main]
    hot_own = key_hot[main : main + rows]
    hot_par = key_hot[main + rows :]
    row_bias = mm(row_hot, table_ref[0], ROW_COL).astype(BF16)
    q_ext = jnp.concatenate([q, row_bias], axis=1)
    k_main_ext = jnp.concatenate([k_main, hot_main], axis=1)
    k_own_ext = jnp.concatenate([kv_own_out[:rows], hot_own], axis=1)
    k_par_ext = jnp.concatenate([kv_par_out[:rows], hot_par], axis=1)
    v_own = kv_own_out[rows:]
    v_par = kv_par_out[rows:]

    def stacked(a, own, par, contract):
        return jnp.concatenate([mm(a[:rows], own, contract), mm(a[rows:], par, contract)], axis=0)

    s_main = mm(q_ext, k_main_ext, ROW_ROW) * inv_scale
    s_out = stacked(q_ext, k_own_ext, k_par_ext, ROW_ROW) * inv_scale
    peak = jnp.maximum(
        jnp.max(s_main, axis=1, keepdims=True), jnp.max(s_out, axis=1, keepdims=True)
    )
    e_main = jnp.exp(s_main - peak)
    e_out = jnp.exp(s_out - peak)
    norm = 1.0 / (
        jnp.sum(e_main, axis=1, keepdims=True) + jnp.sum(e_out, axis=1, keepdims=True)
    )
    p_main = e_main * norm
    p_out = e_out * norm
    pb_main = p_main.astype(BF16)
    pb_out = p_out.astype(BF16)
    mixed = mm(pb_main, v_main, ROW_COL) + stacked(pb_out, v_own, v_par, ROW_COL)
    attended = jnp.where(keep, mixed, 0.0).astype(BF16)
    delta = jnp.sum(g.astype(F32) * mixed, axis=1, keepdims=True)
    d_main = p_main * (mm(g, v_main, ROW_ROW) - delta)
    d_out = p_out * (stacked(g, v_own, v_par, ROW_ROW) - delta)
    db_main = d_main.astype(BF16)
    db_out = d_out.astype(BF16)
    dl_main = (d_main - db_main.astype(F32)).astype(BF16)
    dl_out = (d_out - db_out.astype(F32)).astype(BF16)
    q_terms = mm(db_main, k_main_ext, ROW_COL) + stacked(db_out, k_own_ext, k_par_ext, ROW_COL)
    grad_q = (q_terms[:, :LANES] * inv_scale).astype(BF16)
    by_level = q_terms[:, LANES:] + (
        mm(dl_main, hot_main, ROW_COL) + stacked(dl_out, hot_own, hot_par, ROW_COL)
    )
    bias = lax.dot_general(
        row_hot.astype(F32),
        by_level,
        (COL_COL, ((), ())),
        precision=lax.Precision.HIGHEST,
        preferred_element_type=F32,
    )
    lane = lax.broadcasted_iota(jnp.int32, bias.shape, 1)
    bias = jnp.where(lane < SLOT, bias, 0.0)
    bias = pltpu.roll(bias, step * SLOT, 1)

    @pl.when(step == 0)
    def _():
        bias_ref[...] = bias

    @pl.when(step > 0)
    def _():
        bias_ref[...] = bias_ref[...] + bias

    gk_main = (mm(db_main, q, COL_COL) * inv_scale).astype(BF16)
    gv_main = mm(pb_main, g, COL_COL).astype(BF16)
    gk_own = (mm(db_out[:rows], q[:rows], COL_COL) * inv_scale).astype(BF16)
    gk_par = (mm(db_out[rows:], q[rows:], COL_COL) * inv_scale).astype(BF16)
    gv_own = mm(pb_out[:rows], g[:rows], COL_COL).astype(BF16)
    gv_par = mm(pb_out[rows:], g[rows:], COL_COL).astype(BF16)
    for place, ref in ((0, own_ref), (1, par_ref)):
        here = slice(place * rows, (place + 1) * rows)
        there = slice(total + place * rows, total + (place + 1) * rows)
        ref[0 * rows : 1 * rows] = attended[here]
        ref[1 * rows : 2 * rows] = grad_q[here]
        ref[2 * rows : 3 * rows] = gk_main[there]
        ref[3 * rows : 4 * rows] = gv_main[there]
    own_out_ref[:rows] = gk_own
    own_out_ref[rows:] = gv_own
    par_out_ref[:rows] = gk_par
    par_out_ref[rows:] = gv_par
    for j, (r, a) in enumerate(places):
        coarse_out[r][a : a + part] = gk_main[j * part : (j + 1) * part]
        coarse_out[r][a + part : a + 2 * part] = gv_main[j * part : (j + 1) * part]


def call_kernel(inv_scale, half, full, pairs, coarse, tables, heads):
    rows, width = full[0].shape
    half_width = width // 2
    steps = heads // 2
    row_hot, key_hot, table, keep = tables

    def mine(h, half_ref):
        return (0, half_ref[0] * steps + h)

    def at(h, half_ref):
        return (0, h)

    def fixed(h, half_ref):
        return (0, 0)

    in_specs = (
        [pl.BlockSpec((rows, LANES), mine)] * 4
        + [pl.BlockSpec((2 * rows, LANES), at)] * 4
        + [pl.BlockSpec((x.shape[0], LANES), at) for x in coarse]
        + [
            pl.BlockSpec(row_hot.shape, fixed),
            pl.BlockSpec(key_hot.shape, fixed),
            pl.BlockSpec((1, SLOT, LANES), lambda h, half_ref: (half_ref[0] * steps + h, 0, 0)),
            pl.BlockSpec(keep.shape, fixed),
        ]
    )
    out_rows = [4 * rows] * 2 + [2 * rows] * 2 + [x.shape[0] for x in coarse]
    out_shape = [jax.ShapeDtypeStruct((r, half_width), BF16) for r in out_rows]
    out_shape.append(jax.ShapeDtypeStruct((SLOT, LANES), F32))
    out_specs = [pl.BlockSpec((r, LANES), at) for r in out_rows]
    out_specs.append(pl.BlockSpec((SLOT, LANES), fixed))
    return pl.pallas_call(
        functools.partial(attention_kernel, inv_scale),
        grid_spec=pltpu.PrefetchScalarGridSpec(
            num_scalar_prefetch=1, grid=(steps,), in_specs=in_specs, out_specs=out_specs
        ),
        out_shape=out_shape,
        compiler_params=pltpu.CompilerParams(
            dimension_semantics=("arbitrary",), vmem_limit_bytes=60 * 1024 * 1024
        ),
        cost_estimate=pl.CostEstimate(
            flops=12 * 2 * rows * 640 * half_width,
            bytes_accessed=10 * 1024 * 1024,
            transcendentals=steps * 2 * rows * 640,
        ),
    )(half, *full, *pairs, *coarse, row_hot, key_hot, table, keep)


def shards(queries, keys, values, grad_out, valid, scale_ids, scale_bias):
    q, k, v, g = queries[0], keys[0], values[0], grad_out[0]
    rows, width = q.shape
    half_width = width // 2
    heads, levels = scale_bias.shape[:2]
    tiles = lax.axis_size("tile")
    depth = tiles // 4
    images = lax.axis_size("batch")
    tile = lax.axis_index("tile")
    core = tile % 2
    inv_scale = 1.0 / math.sqrt(width // heads)

    def send(x, target):
        return lax.ppermute(x, "tile", [(i, target(i)) for i in range(tiles)])

    def to_core(x):
        return send(x, lambda i: i ^ 1)

    def to_side(x):
        return send(x, lambda i: i ^ 2)

    def to_corner(x):
        return send(x, lambda i: i ^ 3)

    def to_depth(x, distance):
        return send(x, lambda i: (i + 4 * distance) % tiles)

    edge = []
    jump = []
    for i in range(tiles):
        near = i + 1 if i % 2 else i - 1
        far = i + 2 if i % 2 else i - 2
        if 0 <= near < tiles:
            edge.append((i, near))
        if 0 <= far < tiles:
            jump.append((i, far))

    def cut(x, which):
        return lax.dynamic_slice_in_dim(x, which * half_width, half_width, 1)

    small = jnp.stack([k[:COARSE], v[:COARSE]])
    small_mine = lax.dynamic_slice_in_dim(small, core * half_width, half_width, 2)
    small_other = lax.dynamic_slice_in_dim(small, (1 - core) * half_width, half_width, 2)
    first = [small_mine, to_core(small_other), to_side(small_mine), to_corner(small_other)]
    group = jnp.concatenate(first, axis=1).reshape(-1, half_width)
    up_two = to_depth(group, -2)
    down_two = to_depth(group, 2)
    four = send(
        jnp.where(core == 0, up_two, down_two),
        lambda i: (i + (8 if i % 2 else -8)) % tiles,
    )
    up_odd = to_depth(jnp.concatenate([group, up_two], axis=0), -1)

    kv_other = jnp.concatenate([cut(k, 1 - core), cut(v, 1 - core)], axis=0)
    kv_mine = jnp.concatenate([cut(k, core), cut(v, core)], axis=0)
    qg_other = jnp.concatenate([cut(q, 1 - core), cut(g, 1 - core)], axis=0)
    kv_other, kv_mine, qg_other, _ = lax.optimization_barrier((kv_other, kv_mine, qg_other, group))
    kv_own_out = lax.ppermute(kv_other, "tile", edge)
    kv_par_out = lax.ppermute(kv_mine, "tile", jump)
    kv_par = to_core(kv_other)
    qg_par = to_core(qg_other)
    down_pair = jnp.concatenate([group, down_two], axis=0)
    down_pair, kv_own_out = lax.optimization_barrier((down_pair, kv_own_out))
    down_odd = to_depth(down_pair, 1)
    coarse = [group, up_two, down_two, four, up_odd, down_odd]

    valid_grid = valid[0].reshape(tiles, rows)
    scale_grid = scale_ids.reshape(tiles, rows)
    level_grid = jnp.where(valid_grid > 0, scale_grid, levels)
    inner = jnp.arange(rows, dtype=jnp.int32)
    fine_grid = jnp.where(inner[None, :] >= COARSE, level_grid, levels)
    near_grid = jnp.pad(fine_grid, ((1, 1), (0, 0)), constant_values=levels)
    partner = tile ^ 1
    outward = 2 * core - 1

    def line(grid, index):
        return lax.dynamic_index_in_dim(grid, index, 0, keepdims=False)

    z_here = tile // 4
    spots = jnp.stack([((z_here + d) % depth) * 4 + (j ^ (tile % 4)) for d in OFFSETS for j in range(4)])
    pick = (spots[:, None] == jnp.arange(tiles, dtype=jnp.int32)[None, :]).astype(F32)
    coarse_level = jnp.dot(
        pick, level_grid[:, :COARSE].astype(F32), precision=lax.Precision.HIGHEST
    ).astype(jnp.int32)
    key_level = jnp.concatenate(
        [
            coarse_level.reshape(-1),
            line(near_grid, tile + 1),
            line(near_grid, partner + 1),
            line(near_grid, tile + 1 + outward),
            line(near_grid, partner + 1 - outward),
        ]
    )
    column = jnp.arange(LANES, dtype=jnp.int32)
    key_hot = (
        (key_level[:, None] == (column % SLOT)[None, :]) & (column < 3 * SLOT)[None, :]
    ).astype(BF16)
    row_level = jnp.concatenate([line(scale_grid, tile), line(scale_grid, partner)])
    row_hot = (row_level[:, None] == jnp.arange(SLOT, dtype=jnp.int32)[None, :]).astype(BF16)
    keep = jnp.concatenate([line(valid_grid, tile), line(valid_grid, partner)]).astype(F32)[:, None]

    level_ids = jnp.arange(levels, dtype=jnp.int32)
    scaled = jnp.where(
        (level_ids[None, :] <= level_ids[:, None])[None], scale_bias / inv_scale, MASKED
    )
    scaled = jnp.pad(
        scaled,
        ((0, 0), (0, SLOT - levels), (0, SLOT - levels)),
        constant_values=MASKED,
    )
    parts = []
    rest = scaled
    for _ in range(3):
        piece = lax.reduce_precision(rest, 8, 7)
        parts.append(piece)
        rest = rest - piece
    table = jnp.pad(
        jnp.concatenate(parts, axis=2), ((0, 0), (0, 0), (0, LANES - 3 * SLOT))
    ).astype(BF16)

    results = call_kernel(
        inv_scale,
        core.reshape(1),
        (q, k, v, g),
        (kv_par, qg_par, kv_own_out, kv_par_out),
        coarse,
        (row_hot, key_hot, table, keep),
        heads,
    )
    own, par, own_out, par_out = results[:4]
    here, up_two, down_two, four, up_odd, down_odd = results[4:10]
    bias = results[10]

    def wide(x):
        return x.astype(F32)

    def xor_sum(x, axis, count, bits):
        got = [lax.ppermute(x, axis, [(i, i ^ b) for i in range(count)]) for b in bits]
        return sum(got, x)

    both = ("batch", "tile")
    zero = jnp.zeros((), F32)
    block = here.shape[0]
    back_other = lax.ppermute(own_out, "tile", edge)
    back_mine = lax.ppermute(par_out, "tile", [(b, a) for a, b in jump])
    other = to_core(par)
    up_odd = to_depth(up_odd, 1)
    down_odd = to_depth(down_odd, -1)
    four = send(four, lambda i: (i + (-8 if i % 2 else 8)) % tiles)
    bias = xor_sum(bias, "tile", tiles, (4, 8, 12))
    up_odd, down_odd, four, bias = lax.optimization_barrier((up_odd, down_odd, four, bias))
    up_two = wide(up_two) + wide(up_odd[block:]) + jnp.where(core == 0, wide(four), zero)
    down_two = wide(down_two) + wide(down_odd[block:]) + jnp.where(core == 1, wide(four), zero)
    up_two = to_depth(up_two.astype(BF16), 2)
    down_two = to_depth(down_two.astype(BF16), -2)
    bias = xor_sum(bias, "tile", tiles, (16, 2, 18))
    up_two, down_two, bias = lax.optimization_barrier((up_two, down_two, bias))
    summed = wide(here) + wide(up_odd[:block]) + wide(down_odd[:block])
    summed = summed + wide(up_two) + wide(down_two)
    summed = summed.reshape(2, 4, COARSE, half_width)
    narrow = summed.astype(BF16)
    quad = [to_core(narrow[:, 1]), to_side(narrow[:, 2]), to_corner(narrow[:, 3])]
    bias, back_other = lax.optimization_barrier((bias, back_other))
    bias = xor_sum(bias, "batch", images, (1, 2, 3))
    quad[0], quad[1], quad[2], bias = lax.optimization_barrier((*quad, bias))
    coarse_mine = summed[:, 0] + wide(quad[1])
    coarse_other = wide(quad[0]) + wide(quad[2])
    every = images * tiles
    half_count = every // 2
    same = lax.ppermute(bias, both, [(i, i ^ half_count) for i in range(every)])
    swap = to_core(bias)
    cross = lax.ppermute(bias, both, [(i, i ^ half_count ^ 1) for i in range(every)])
    mine_bias = bias + same
    other_bias = swap + cross
    bias_halves = jnp.where(
        core == 0, jnp.stack([mine_bias, other_bias]), jnp.stack([other_bias, mine_bias])
    )
    grad_bias = (
        bias_halves.reshape(2, SLOT, heads // 2, SLOT)
        .transpose(0, 2, 1, 3)
        .reshape(heads, SLOT, SLOT)[:, :levels, :levels]
    )

    def joined(mine, other_half):
        return jnp.where(
            core == 0,
            jnp.concatenate([mine, other_half], axis=-1),
            jnp.concatenate([other_half, mine], axis=-1),
        )

    attended = joined(own[:rows], other[:rows])
    grad_q = joined(own[rows : 2 * rows], other[rows : 2 * rows])
    fine_mine = wide(own[2 * rows :]) + wide(back_mine)
    fine_other = wide(other[2 * rows :]) + wide(back_other)
    fine = joined(fine_mine, fine_other).reshape(2, rows, width)
    coarse_rows = joined(coarse_mine, coarse_other)
    grads = jnp.concatenate([coarse_rows, fine[:, COARSE:]], axis=1).astype(BF16)
    return (attended[None], grad_q[None], grads[0][None], grads[1][None], grad_bias)


def solution(mesh):
    block = P("batch", "tile", None)
    return jax.shard_map(
        shards,
        mesh=mesh,
        in_specs=(block, block, block, block, P("batch", None), P(), P()),
        out_specs=(block, block, block, block, P()),
        check_vma=False,
    )
```

```python
import functools
import math

import jax
import jax.numpy as jnp
from jax import lax
from jax.experimental import pallas as pl
from jax.experimental.pallas import tpu as pltpu
from jax.sharding import PartitionSpec as P

COARSE = 8
MASKED = -1e30
LANES = 128
SLOT = 16
PER_STEP = 2
BF16 = jnp.bfloat16
F32 = jnp.float32
OFFSETS = (0, 2, -2, 4, 1, 3, -1, -3)


def after(x, *done):
    return lax.optimization_barrier((x, *done))[0]


def mm(a, b, contract):
    return lax.dot_general(a, b, (contract, ((), ())), preferred_element_type=F32)


ROW_COL = ((1,), (0,))
ROW_ROW = ((1,), (1,))
COL_COL = ((0,), (0,))


def split_sum(x):
    lane = lax.broadcasted_iota(jnp.int32, x.shape, 1)
    high = x.astype(BF16).astype(F32)
    rest = x - high
    mid = rest.astype(BF16).astype(F32)
    low = rest - mid
    kept = jnp.where(lane < SLOT, high, jnp.where(lane < 2 * SLOT, mid, low))
    return jnp.where(lane < 3 * SLOT, kept, 0.0).astype(BF16)


def whole_sum(x):
    lane = lax.broadcasted_iota(jnp.int32, x.shape, 1)
    total = x + pltpu.roll(x, LANES - SLOT, 1) + pltpu.roll(x, LANES - 2 * SLOT, 1)
    return jnp.where(lane < SLOT, total, 0.0)


def resplit(x):
    total = whole_sum(x)
    return split_sum(total + pltpu.roll(total, SLOT, 1) + pltpu.roll(total, 2 * SLOT, 1))


def wide(x):
    return x.astype(F32)


def merge_kernel(half_ref, up_ref, down_ref, four_ref, up_odd_ref, down_odd_ref, up_out, down_out):
    block = up_ref.shape[0]
    across = wide(four_ref[...])
    upper = half_ref[0] == 0
    for ref, odd, far, out in (
        (up_ref, up_odd_ref, upper, up_out),
        (down_ref, down_odd_ref, jnp.logical_not(upper), down_out),
    ):
        total = wide(ref[...]) + wide(odd[block:]) + jnp.where(far, across, 0.0)
        out[: block - SLOT] = total[: block - SLOT].astype(BF16)
        for h in range(0, total.shape[1], LANES):
            out[block - SLOT :, h : h + LANES] = resplit(total[block - SLOT :, h : h + LANES])


def quad_kernel(here_ref, up_ref, down_ref, up_two_ref, down_two_ref, keep_out, *outs):
    block = here_ref.shape[0]
    total = wide(here_ref[...]) + wide(up_ref[:block]) + wide(down_ref[:block])
    total = total + wide(up_two_ref[...]) + wide(down_two_ref[...])
    part = (block - SLOT) // 2
    pieces = [
        jnp.concatenate(
            [total[j * COARSE : (j + 1) * COARSE], total[part + j * COARSE : part + (j + 1) * COARSE]],
            axis=0,
        )
        for j in range(4)
    ]
    tail = total[block - SLOT :]
    keep_out[: 2 * COARSE] = pieces[0]
    keep_out[2 * COARSE :] = tail
    bias = [resplit(tail[:, h : h + LANES]) for h in range(0, total.shape[1], LANES)]
    bias = jnp.concatenate(bias, axis=1)
    for piece, out in zip(pieces[1:], outs):
        out[: 2 * COARSE] = piece.astype(BF16)
        out[2 * COARSE :] = bias


def finish_kernel(half_ref, keep_ref, core_ref, side_ref, corner_ref, rows_out, bias_out):
    mine = keep_ref[...] + wide(side_ref[...])
    other = wide(core_ref[...]) + wide(corner_ref[...])
    first = half_ref[0] == 0
    low = jnp.where(first, mine, other)
    high = jnp.where(first, other, mine)
    rows_out[...] = jnp.concatenate([low[: 2 * COARSE], high[: 2 * COARSE]], axis=1).astype(BF16)
    for i, x in enumerate((low, high)):
        packed = jnp.zeros((SLOT, LANES), F32)
        for h in range(LANES // SLOT):
            one = whole_sum(x[2 * COARSE :, h * LANES : (h + 1) * LANES])
            packed = packed + (pltpu.roll(one, h * SLOT, 1) if h else one)
        bias_out[i * SLOT : (i + 1) * SLOT] = packed


def small_call(kernel, half, arrays, out_shape):
    smem = [pl.BlockSpec(memory_space=pltpu.SMEM)] if half is not None else []
    args = [half] if half is not None else []
    return pl.pallas_call(
        kernel,
        in_specs=smem + [pl.BlockSpec(memory_space=pltpu.VMEM)] * len(arrays),
        out_specs=[pl.BlockSpec(memory_space=pltpu.VMEM)] * len(out_shape),
        out_shape=out_shape,
        cost_estimate=pl.CostEstimate(flops=10**6, bytes_accessed=10**6, transcendentals=0),
    )(*args, *arrays)


def attention_kernel(inv_scale, half_ref, *refs):
    (q_ref, k_ref, v_ref, g_ref, kv_par, qg_par, kv_own_out, kv_par_out) = refs[:8]
    coarse_refs = refs[8:14]
    row_hot_ref, key_hot_ref, table_ref, keep_ref = refs[14:18]
    own_ref, par_ref, own_out_ref, par_out_ref = refs[18:22]
    coarse_out = refs[22:28]
    rows = q_ref.shape[0]
    part = coarse_refs[0].shape[0] // 2
    places = [(r, a) for r in range(len(coarse_refs)) for a in range(0, coarse_refs[r].shape[0], 2 * part)]
    total = part * len(places)
    keep = keep_ref[...] > 0.0
    row_hot = row_hot_ref[...]
    key_hot = key_hot_ref[...]

    def one_head(head):
        lanes = slice(head * LANES, (head + 1) * LANES)
        q = jnp.concatenate([q_ref[:, lanes], qg_par[:rows, lanes]], axis=0)
        g_all = jnp.concatenate([g_ref[:, lanes], qg_par[rows:, lanes]], axis=0)
        g = jnp.where(keep, g_all.astype(F32), 0.0).astype(BF16)
        k_main = jnp.concatenate([coarse_refs[r][a : a + part, lanes] for r, a in places] + [k_ref[:, lanes], kv_par[:rows, lanes]], axis=0)
        v_main = jnp.concatenate([coarse_refs[r][a + part : a + 2 * part, lanes] for r, a in places] + [v_ref[:, lanes], kv_par[rows:, lanes]], axis=0)
        main = k_main.shape[0]
        hot_main = key_hot[:main]
        hot_own = key_hot[main : main + rows]
        hot_par = key_hot[main + rows :]
        row_bias = mm(row_hot, table_ref[head], ROW_COL).astype(BF16)
        q_ext = jnp.concatenate([q, row_bias], axis=1)
        k_main_ext = jnp.concatenate([k_main, hot_main], axis=1)
        k_own_ext = jnp.concatenate([kv_own_out[:rows, lanes], hot_own], axis=1)
        k_par_ext = jnp.concatenate([kv_par_out[:rows, lanes], hot_par], axis=1)
        v_own = kv_own_out[rows:, lanes]
        v_par = kv_par_out[rows:, lanes]

        def stacked(a, own, par, contract):
            return jnp.concatenate([mm(a[:rows], own, contract), mm(a[rows:], par, contract)], axis=0)

        to_two = inv_scale * math.log2(math.e)
        s_main = mm(q_ext, k_main_ext, ROW_ROW)
        s_out = stacked(q_ext, k_own_ext, k_par_ext, ROW_ROW)
        gp_main = mm(g, v_main, ROW_ROW)
        gp_out = stacked(g, v_own, v_par, ROW_ROW)
        yield
        peak = jnp.maximum(
            jnp.max(s_main, axis=1, keepdims=True), jnp.max(s_out, axis=1, keepdims=True)
        )
        e_main = jnp.exp2((s_main - peak) * to_two)
        e_out = jnp.exp2((s_out - peak) * to_two)
        yield
        norm = 1.0 / (
            jnp.sum(e_main, axis=1, keepdims=True) + jnp.sum(e_out, axis=1, keepdims=True)
        )
        p_main = e_main * norm
        p_out = e_out * norm
        pb_main = p_main.astype(BF16)
        pb_out = p_out.astype(BF16)
        mixed = mm(pb_main, v_main, ROW_COL) + stacked(pb_out, v_own, v_par, ROW_COL)
        yield
        attended = jnp.where(keep, mixed, 0.0).astype(BF16)
        delta = jnp.sum(g.astype(F32) * mixed, axis=1, keepdims=True)
        d_main = p_main * (gp_main - delta)
        d_out = p_out * (gp_out - delta)
        db_main = d_main.astype(BF16)
        db_out = d_out.astype(BF16)
        dl_main = (d_main - db_main.astype(F32)).astype(BF16)
        dl_out = (d_out - db_out.astype(F32)).astype(BF16)
        yield
        q_terms = mm(db_main, k_main_ext, ROW_COL) + stacked(db_out, k_own_ext, k_par_ext, ROW_COL)
        grad_q = (q_terms[:, :LANES] * inv_scale).astype(BF16)
        by_level = q_terms[:, LANES:] + (
            mm(dl_main, hot_main, ROW_COL) + stacked(dl_out, hot_own, hot_par, ROW_COL)
        )
        bias = lax.dot_general(
            row_hot.astype(F32),
            by_level,
            (COL_COL, ((), ())),
            precision=lax.Precision.HIGHEST,
            preferred_element_type=F32,
        )
        bias = split_sum(bias)
        yield
        gk_main = (mm(db_main, q, COL_COL) * inv_scale).astype(BF16)
        gv_main = mm(pb_main, g, COL_COL).astype(BF16)
        gk_own = (mm(db_out[:rows], q[:rows], COL_COL) * inv_scale).astype(BF16)
        gk_par = (mm(db_out[rows:], q[rows:], COL_COL) * inv_scale).astype(BF16)
        gv_own = mm(pb_out[:rows], g[:rows], COL_COL).astype(BF16)
        gv_par = mm(pb_out[rows:], g[rows:], COL_COL).astype(BF16)
        for place, ref in ((0, own_ref), (1, par_ref)):
            here = slice(place * rows, (place + 1) * rows)
            there = slice(total + place * rows, total + (place + 1) * rows)
            ref[0 * rows : 1 * rows, lanes] = attended[here]
            ref[1 * rows : 2 * rows, lanes] = grad_q[here]
            ref[2 * rows : 3 * rows, lanes] = gk_main[there]
            ref[3 * rows : 4 * rows, lanes] = gv_main[there]
        own_out_ref[:rows, lanes] = gk_own
        own_out_ref[rows:, lanes] = gv_own
        par_out_ref[:rows, lanes] = gk_par
        par_out_ref[rows:, lanes] = gv_par
        for j, (r, a) in enumerate(places):
            a = a // (2 * part) * (2 * part + SLOT)
            coarse_out[r][a : a + part, lanes] = gk_main[j * part : (j + 1) * part]
            coarse_out[r][a + part : a + 2 * part, lanes] = gv_main[j * part : (j + 1) * part]
            coarse_out[r][a + 2 * part : a + 2 * part + SLOT, lanes] = bias

    waiting = [one_head(head) for head in range(table_ref.shape[0])]
    running = []
    while waiting or running:
        if waiting and len(running) < 2:
            running.append(waiting.pop(0))
        for work in list(running):
            if next(work, running) is running:
                running.remove(work)


def call_kernel(inv_scale, half, full, pairs, coarse, tables, heads):
    rows, width = full[0].shape
    half_width = width // 2
    steps = heads // 2 // PER_STEP
    lanes = PER_STEP * LANES
    row_hot, key_hot, table, keep = tables

    def mine(h, half_ref):
        return (0, half_ref[0] * steps + h)

    def at(h, half_ref):
        return (0, h)

    def fixed(h, half_ref):
        return (0, 0)

    in_specs = (
        [pl.BlockSpec((rows, lanes), mine)] * 4
        + [pl.BlockSpec((2 * rows, lanes), at)] * 4
        + [pl.BlockSpec((x.shape[0], lanes), at) for x in coarse]
        + [
            pl.BlockSpec(row_hot.shape, fixed),
            pl.BlockSpec(key_hot.shape, fixed),
            pl.BlockSpec((PER_STEP, SLOT, LANES), lambda h, half_ref: (half_ref[0] * steps + h, 0, 0)),
            pl.BlockSpec(keep.shape, fixed),
        ]
    )
    blocks = [x.shape[0] // coarse[0].shape[0] for x in coarse]
    out_rows = [4 * rows] * 2 + [2 * rows] * 2 + [n * (coarse[0].shape[0] + SLOT) for n in blocks]
    out_shape = [jax.ShapeDtypeStruct((r, half_width), BF16) for r in out_rows]
    out_specs = [pl.BlockSpec((r, lanes), at) for r in out_rows]
    return pl.pallas_call(
        functools.partial(attention_kernel, inv_scale),
        grid_spec=pltpu.PrefetchScalarGridSpec(
            num_scalar_prefetch=1, grid=(steps,), in_specs=in_specs, out_specs=out_specs
        ),
        out_shape=out_shape,
        compiler_params=pltpu.CompilerParams(
            dimension_semantics=("arbitrary",), vmem_limit_bytes=60 * 1024 * 1024
        ),
        cost_estimate=pl.CostEstimate(
            flops=12 * 2 * rows * 640 * half_width,
            bytes_accessed=10 * 1024 * 1024,
            transcendentals=heads * rows * 640,
        ),
    )(half, *full, *pairs, *coarse, row_hot, key_hot, table, keep)


def shards(queries, keys, values, grad_out, valid, scale_ids, scale_bias):
    q, k, v, g = queries[0], keys[0], values[0], grad_out[0]
    rows, width = q.shape
    half_width = width // 2
    heads, levels = scale_bias.shape[:2]
    tiles = lax.axis_size("tile")
    depth = tiles // 4
    images = lax.axis_size("batch")
    tile = lax.axis_index("tile")
    core = tile % 2
    inv_scale = 1.0 / math.sqrt(width // heads)
    half = core.reshape(1)

    def send(x, target):
        return lax.ppermute(x, "tile", [(i, target(i)) for i in range(tiles)])

    def to_core(x):
        return send(x, lambda i: i ^ 1)

    def to_side(x):
        return send(x, lambda i: i ^ 2)

    def to_corner(x):
        return send(x, lambda i: i ^ 3)

    def to_depth(x, distance):
        return send(x, lambda i: (i + 4 * distance) % tiles)

    edge = [(i, (i + 1 if i % 2 else i - 1) % tiles) for i in range(tiles)]
    jump = [(i, (i + 2 if i % 2 else i - 2) % tiles) for i in range(tiles)]

    def cut(x, which):
        return lax.dynamic_slice_in_dim(x, which * half_width, half_width, 1)

    def small(which):
        start, size = (0, which * half_width), (COARSE, half_width)
        return jnp.stack([lax.dynamic_slice(k, start, size), lax.dynamic_slice(v, start, size)])

    small_mine, small_other = small(core), small(1 - core)
    first = [small_mine, to_core(small_other), to_side(small_mine), to_corner(small_other)]
    kv_other = jnp.concatenate([cut(k, 1 - core), cut(v, 1 - core)], axis=0)
    kv_mine = jnp.concatenate([cut(k, core), cut(v, core)], axis=0)
    qg_other = jnp.concatenate([cut(q, 1 - core), cut(g, 1 - core)], axis=0)
    first[1], first[3], kv_other = lax.optimization_barrier((first[1], first[3], kv_other))
    kv_own_out = lax.ppermute(kv_other, "tile", edge)
    group = jnp.concatenate(first, axis=1).reshape(-1, half_width)
    kv_mine, qg_other, group = lax.optimization_barrier((kv_mine, qg_other, group))
    kv_par_out = lax.ppermute(kv_mine, "tile", jump)
    kv_par = to_core(kv_other)
    qg_par = to_core(qg_other)
    up_two = to_depth(group, -2)
    down_two = to_depth(group, 2)
    up_odd = to_depth(jnp.concatenate([group, up_two], axis=0), -1)
    down_odd = to_depth(jnp.concatenate([group, down_two], axis=0), 1)
    far = jnp.where(core == 0, up_two, down_two)
    far, kv_own_out = lax.optimization_barrier((far, kv_own_out))
    four = send(far, lambda i: (i + (8 if i % 2 else -8)) % tiles)
    coarse = [group, up_two, down_two, four, up_odd, down_odd]

    valid_grid = valid[0].reshape(tiles, rows)
    scale_grid = scale_ids.reshape(tiles, rows)
    level_grid = jnp.where(valid_grid > 0, scale_grid, levels)
    inner = jnp.arange(rows, dtype=jnp.int32)
    fine_grid = jnp.where(inner[None, :] >= COARSE, level_grid, levels)
    near_grid = jnp.pad(fine_grid, ((1, 1), (0, 0)), constant_values=levels)
    partner = tile ^ 1
    outward = 2 * core - 1

    def line(grid, index):
        return lax.dynamic_index_in_dim(grid, index, 0, keepdims=False)

    z_here = tile // 4
    spots = jnp.stack([((z_here + d) % depth) * 4 + (j ^ (tile % 4)) for d in OFFSETS for j in range(4)])
    pick = (spots[:, None] == jnp.arange(tiles, dtype=jnp.int32)[None, :]).astype(F32)
    coarse_level = jnp.dot(
        pick, level_grid[:, :COARSE].astype(F32), precision=lax.Precision.HIGHEST
    ).astype(jnp.int32)
    key_level = jnp.concatenate(
        [
            coarse_level.reshape(-1),
            line(near_grid, tile + 1),
            line(near_grid, partner + 1),
            line(near_grid, tile + 1 + outward),
            line(near_grid, partner + 1 - outward),
        ]
    )
    column = jnp.arange(LANES, dtype=jnp.int32)
    key_hot = (
        (key_level[:, None] == (column % SLOT)[None, :]) & (column < 3 * SLOT)[None, :]
    ).astype(BF16)
    row_level = jnp.concatenate([line(scale_grid, tile), line(scale_grid, partner)])
    row_hot = (row_level[:, None] == jnp.arange(SLOT, dtype=jnp.int32)[None, :]).astype(BF16)
    keep = jnp.concatenate([line(valid_grid, tile), line(valid_grid, partner)]).astype(F32)[:, None]

    level_ids = jnp.arange(levels, dtype=jnp.int32)
    scaled = jnp.where(
        (level_ids[None, :] <= level_ids[:, None])[None], scale_bias / inv_scale, MASKED
    )
    scaled = jnp.pad(
        scaled,
        ((0, 0), (0, SLOT - levels), (0, SLOT - levels)),
        constant_values=MASKED,
    )
    parts = []
    rest = scaled
    for _ in range(3):
        piece = lax.reduce_precision(rest, 8, 7)
        parts.append(piece)
        rest = rest - piece
    table = jnp.pad(
        jnp.concatenate(parts, axis=2), ((0, 0), (0, 0), (0, LANES - 3 * SLOT))
    ).astype(BF16)

    results = call_kernel(
        inv_scale,
        half,
        (q, k, v, g),
        (kv_par, qg_par, kv_own_out, kv_par_out),
        coarse,
        (row_hot, key_hot, table, keep),
        heads,
    )
    own, par, own_out, par_out = results[:4]
    here, up_two, down_two, four, up_odd, down_odd = results[4:10]

    def joined(mine, other_half):
        return jnp.where(
            core == 0,
            jnp.concatenate([mine, other_half], axis=-1),
            jnp.concatenate([other_half, mine], axis=-1),
        )

    every = images * tiles

    def flipped(x, mask):
        return lax.ppermute(x, ("batch", "tile"), [(i, i ^ mask) for i in range(every)])

    block, columns = here.shape

    def like(count, dtype):
        return jax.ShapeDtypeStruct((count, columns), dtype)

    def beside(pairs):
        return [p for p in pairs if p[0] // 4 == p[1] // 4], [p for p in pairs if p[0] // 4 != p[1] // 4]

    edge_y, edge_z = beside(edge)
    jump_y, jump_z = beside([(b, a) for a, b in jump])
    jump_y, jump_z = jump_y + [(i, i ^ 1) for i, _ in jump_z], jump_z + [(i, i ^ 1) for i, _ in jump_y]
    middle = (tile % 4 == 1) | (tile % 4 == 2)
    other_y = lax.ppermute(own_out, "tile", edge_y)
    mine_y = lax.ppermute(par_out, "tile", jump_y)
    other = to_core(par)
    up_odd = to_depth(up_odd, 1)
    down_odd = to_depth(down_odd, -1)
    four = send(four, lambda i: (i + (-8 if i % 2 else 8)) % tiles)
    up_odd, down_odd, four, own_out, par_out, other_y = lax.optimization_barrier(
        (up_odd, down_odd, four, own_out, par_out, other_y)
    )
    up_two, down_two = small_call(
        merge_kernel, half, (up_two, down_two, four, up_odd, down_odd), [like(block, BF16)] * 2
    )
    own_out, par_out, up_two, down_two = lax.optimization_barrier((own_out, par_out, up_two, down_two))
    other_z = lax.ppermute(own_out, "tile", edge_z)
    mine_z = lax.ppermute(par_out, "tile", jump_z)
    up_two = to_depth(up_two, 2)
    down_two = to_depth(down_two, -2)
    up_two, down_two, mine_y, other = lax.optimization_barrier((up_two, down_two, mine_y, other))
    kept, *quad = small_call(
        quad_kernel,
        None,
        (here, up_odd, down_odd, up_two, down_two),
        [like(2 * COARSE + SLOT, F32)] + [like(2 * COARSE + SLOT, BF16)] * 3,
    )
    quad = [to_core(quad[0]), to_side(quad[1]), to_corner(quad[2])]
    attended = joined(own[:rows], other[:rows])
    grad_q = joined(own[rows : 2 * rows], other[rows : 2 * rows])
    *quad, other_z = lax.optimization_barrier((*quad, other_z))
    fine_other = wide(other[2 * rows :]) + wide(other_y) + wide(other_z)
    coarse_rows, bias = small_call(
        finish_kernel,
        half,
        (kept, *quad),
        [
            jax.ShapeDtypeStruct((2 * COARSE, width), BF16),
            jax.ShapeDtypeStruct((2 * SLOT, LANES), F32),
        ],
    )
    bias = sum([flipped(bias, m * tiles) for m in (1, 2, 3)], bias)
    bias, mine_z, attended, grad_q = lax.optimization_barrier((bias, mine_z, attended, grad_q))
    bias = bias + flipped(bias, 4 * tiles)
    fine_mine = wide(own[2 * rows :]) + wide(jnp.where(middle, mine_y, mine_z))
    fine = joined(fine_mine, fine_other).astype(BF16)
    grad_bias = (
        bias.reshape(2, SLOT, heads // 2, SLOT)
        .transpose(0, 2, 1, 3)
        .reshape(heads, SLOT, SLOT)[:, :levels, :levels]
    )

    coarse_rows = coarse_rows.reshape(2, COARSE, width)
    fine = fine.reshape(2, rows, width)
    grads = jnp.concatenate([coarse_rows, fine[:, COARSE:]], axis=1)
    return (attended[None], grad_q[None], grads[0][None], grads[1][None], grad_bias)


def solution(mesh):
    block = P("batch", "tile", None)
    return jax.shard_map(
        shards,
        mesh=mesh,
        in_specs=(block, block, block, block, P("batch", None), P(), P()),
        out_specs=(block, block, block, block, P()),
        check_vma=False,
    )
```

```python
import functools
import math

import jax
import jax.numpy as jnp
from jax import lax
from jax.experimental import pallas as pl
from jax.experimental.pallas import tpu as pltpu
from jax.sharding import PartitionSpec as P

COARSE = 8
MASKED = -1e30
LANES = 128
SLOT = 16
PER_STEP = 2
BF16 = jnp.bfloat16
F32 = jnp.float32
OFFSETS = (0, 2, -2, 4, 1, 3, -1, -3)


def after(x, *done):
    return lax.optimization_barrier((x, *done))[0]


def mm(a, b, contract):
    return lax.dot_general(a, b, (contract, ((), ())), preferred_element_type=F32)


ROW_COL = ((1,), (0,))
ROW_ROW = ((1,), (1,))
COL_COL = ((0,), (0,))


def split_sum(x):
    lane = lax.broadcasted_iota(jnp.int32, x.shape, 1)
    high = x.astype(BF16).astype(F32)
    rest = x - high
    mid = rest.astype(BF16).astype(F32)
    low = rest - mid
    kept = jnp.where(lane < SLOT, high, jnp.where(lane < 2 * SLOT, mid, low))
    return jnp.where(lane < 3 * SLOT, kept, 0.0).astype(BF16)


def whole_sum(x):
    lane = lax.broadcasted_iota(jnp.int32, x.shape, 1)
    total = x + pltpu.roll(x, LANES - SLOT, 1) + pltpu.roll(x, LANES - 2 * SLOT, 1)
    return jnp.where(lane < SLOT, total, 0.0)


def resplit(x):
    total = whole_sum(x)
    return split_sum(total + pltpu.roll(total, SLOT, 1) + pltpu.roll(total, 2 * SLOT, 1))


def wide(x):
    return x.astype(F32)


def merge_kernel(half_ref, up_ref, down_ref, four_ref, up_odd_ref, down_odd_ref, up_out, down_out):
    block = up_ref.shape[0]
    across = wide(four_ref[...])
    upper = half_ref[0] == 0
    for ref, odd, far, out in (
        (up_ref, up_odd_ref, upper, up_out),
        (down_ref, down_odd_ref, jnp.logical_not(upper), down_out),
    ):
        total = wide(ref[...]) + wide(odd[block - SLOT :]) + jnp.where(far, across, 0.0)
        out[: block - SLOT] = total[: block - SLOT].astype(BF16)
        for h in range(0, total.shape[1], LANES):
            out[block - SLOT :, h : h + LANES] = resplit(total[block - SLOT :, h : h + LANES])


def quad_kernel(here_ref, up_ref, down_ref, up_two_ref, down_two_ref, keep_out, *outs):
    block = here_ref.shape[0]
    both = slice(0, block - SLOT), slice(2 * (block - SLOT), 2 * (block - SLOT) + SLOT)
    up = jnp.concatenate([wide(up_ref[rows]) for rows in both], axis=0)
    down = jnp.concatenate([wide(down_ref[rows]) for rows in both], axis=0)
    total = wide(here_ref[...]) + up + down
    total = total + wide(up_two_ref[...]) + wide(down_two_ref[...])
    part = (block - SLOT) // 2
    pieces = [
        jnp.concatenate(
            [total[j * COARSE : (j + 1) * COARSE], total[part + j * COARSE : part + (j + 1) * COARSE]],
            axis=0,
        )
        for j in range(4)
    ]
    tail = total[block - SLOT :]
    keep_out[: 2 * COARSE] = pieces[0]
    keep_out[2 * COARSE :] = tail
    bias = [resplit(tail[:, h : h + LANES]) for h in range(0, total.shape[1], LANES)]
    bias = jnp.concatenate(bias, axis=1)
    for piece, out in zip(pieces[1:], outs):
        out[: 2 * COARSE] = piece.astype(BF16)
        out[2 * COARSE :] = bias


def finish_kernel(half_ref, keep_ref, core_ref, side_ref, corner_ref, rows_out, bias_out):
    mine = keep_ref[...] + wide(side_ref[...])
    other = wide(core_ref[...]) + wide(corner_ref[...])
    first = half_ref[0] == 0
    low = jnp.where(first, mine, other)
    high = jnp.where(first, other, mine)
    rows_out[...] = jnp.concatenate([low[: 2 * COARSE], high[: 2 * COARSE]], axis=1).astype(BF16)
    for i, x in enumerate((low, high)):
        packed = jnp.zeros((SLOT, LANES), F32)
        for h in range(LANES // SLOT):
            one = whole_sum(x[2 * COARSE :, h * LANES : (h + 1) * LANES])
            packed = packed + (pltpu.roll(one, h * SLOT, 1) if h else one)
        bias_out[i * SLOT : (i + 1) * SLOT] = packed


def small_call(kernel, half, arrays, out_shape):
    smem = [pl.BlockSpec(memory_space=pltpu.SMEM)] if half is not None else []
    args = [half] if half is not None else []
    return pl.pallas_call(
        kernel,
        in_specs=smem + [pl.BlockSpec(memory_space=pltpu.VMEM)] * len(arrays),
        out_specs=[pl.BlockSpec(memory_space=pltpu.VMEM)] * len(out_shape),
        out_shape=out_shape,
        cost_estimate=pl.CostEstimate(flops=10**6, bytes_accessed=10**6, transcendentals=0),
    )(*args, *arrays)


def attention_kernel(inv_scale, half_ref, *refs):
    (q_ref, k_ref, v_ref, g_ref, kv_par, qg_par, kv_own_out, kv_par_out) = refs[:8]
    coarse_refs = refs[8:14]
    row_hot_ref, key_hot_ref, table_ref, keep_ref = refs[14:18]
    own_ref, par_ref, own_out_ref, par_out_ref = refs[18:22]
    coarse_out = refs[22:28]
    rows = q_ref.shape[0]
    part = coarse_refs[0].shape[0] // 2
    places = [(r, a) for r in range(len(coarse_refs)) for a in range(0, coarse_refs[r].shape[0], 2 * part)]
    total = part * len(places)
    keep = keep_ref[...] > 0.0
    row_hot = row_hot_ref[...]
    key_hot = key_hot_ref[...]

    def one_head(head):
        lanes = slice(head * LANES, (head + 1) * LANES)
        q = jnp.concatenate([q_ref[:, lanes], qg_par[:rows, lanes]], axis=0)
        g_all = jnp.concatenate([g_ref[:, lanes], qg_par[rows:, lanes]], axis=0)
        g = jnp.where(keep, g_all.astype(F32), 0.0).astype(BF16)
        k_main = jnp.concatenate([coarse_refs[r][a : a + part, lanes] for r, a in places] + [k_ref[:, lanes], kv_par[:rows, lanes]], axis=0)
        v_main = jnp.concatenate([coarse_refs[r][a + part : a + 2 * part, lanes] for r, a in places] + [v_ref[:, lanes], kv_par[rows:, lanes]], axis=0)
        main = k_main.shape[0]
        hot_main = key_hot[:main]
        hot_own = key_hot[main : main + rows]
        hot_par = key_hot[main + rows :]
        row_bias = mm(row_hot, table_ref[head], ROW_COL).astype(BF16)
        q_ext = jnp.concatenate([q, row_bias], axis=1)
        k_main_ext = jnp.concatenate([k_main, hot_main], axis=1)
        k_own_ext = jnp.concatenate([kv_own_out[:rows, lanes], hot_own], axis=1)
        k_par_ext = jnp.concatenate([kv_par_out[:rows, lanes], hot_par], axis=1)
        v_own = kv_own_out[rows:, lanes]
        v_par = kv_par_out[rows:, lanes]

        def stacked(a, own, par, contract):
            return jnp.concatenate([mm(a[:rows], own, contract), mm(a[rows:], par, contract)], axis=0)

        to_two = inv_scale * math.log2(math.e)
        s_main = mm(q_ext, k_main_ext, ROW_ROW)
        s_out = stacked(q_ext, k_own_ext, k_par_ext, ROW_ROW)
        gp_main = mm(g, v_main, ROW_ROW)
        gp_out = stacked(g, v_own, v_par, ROW_ROW)
        yield
        peak = jnp.maximum(
            jnp.max(s_main, axis=1, keepdims=True), jnp.max(s_out, axis=1, keepdims=True)
        )
        e_main = jnp.exp2((s_main - peak) * to_two)
        e_out = jnp.exp2((s_out - peak) * to_two)
        yield
        norm = 1.0 / (
            jnp.sum(e_main, axis=1, keepdims=True) + jnp.sum(e_out, axis=1, keepdims=True)
        )
        p_main = e_main * norm
        p_out = e_out * norm
        pb_main = p_main.astype(BF16)
        pb_out = p_out.astype(BF16)
        mixed = mm(pb_main, v_main, ROW_COL) + stacked(pb_out, v_own, v_par, ROW_COL)
        yield
        attended = jnp.where(keep, mixed, 0.0).astype(BF16)
        delta = jnp.sum(g.astype(F32) * mixed, axis=1, keepdims=True)
        d_main = p_main * (gp_main - delta)
        d_out = p_out * (gp_out - delta)
        db_main = d_main.astype(BF16)
        db_out = d_out.astype(BF16)
        dl_main = (d_main - db_main.astype(F32)).astype(BF16)
        dl_out = (d_out - db_out.astype(F32)).astype(BF16)
        yield
        q_terms = mm(db_main, k_main_ext, ROW_COL) + stacked(db_out, k_own_ext, k_par_ext, ROW_COL)
        grad_q = (q_terms[:, :LANES] * inv_scale).astype(BF16)
        by_level = q_terms[:, LANES:] + (
            mm(dl_main, hot_main, ROW_COL) + stacked(dl_out, hot_own, hot_par, ROW_COL)
        )
        bias = resplit(mm(row_hot, split_sum(by_level), COL_COL))
        yield
        gk_main = (mm(db_main, q, COL_COL) * inv_scale).astype(BF16)
        gv_main = mm(pb_main, g, COL_COL).astype(BF16)
        gk_own = (mm(db_out[:rows], q[:rows], COL_COL) * inv_scale).astype(BF16)
        gk_par = (mm(db_out[rows:], q[rows:], COL_COL) * inv_scale).astype(BF16)
        gv_own = mm(pb_out[:rows], g[:rows], COL_COL).astype(BF16)
        gv_par = mm(pb_out[rows:], g[rows:], COL_COL).astype(BF16)
        for place, ref in ((0, own_ref), (1, par_ref)):
            here = slice(place * rows, (place + 1) * rows)
            there = slice(total + place * rows, total + (place + 1) * rows)
            ref[0 * rows : 1 * rows, lanes] = attended[here]
            ref[1 * rows : 2 * rows, lanes] = grad_q[here]
            ref[2 * rows : 3 * rows, lanes] = gk_main[there]
            ref[3 * rows : 4 * rows, lanes] = gv_main[there]
        own_out_ref[:rows, lanes] = gk_own
        own_out_ref[rows:, lanes] = gv_own
        par_out_ref[:rows, lanes] = gk_par
        par_out_ref[rows:, lanes] = gv_par
        for ref in coarse_out:
            ref[ref.shape[0] - SLOT :, lanes] = bias
        for j, (r, a) in enumerate(places):
            coarse_out[r][a : a + part, lanes] = gk_main[j * part : (j + 1) * part]
            coarse_out[r][a + part : a + 2 * part, lanes] = gv_main[j * part : (j + 1) * part]

    waiting = [one_head(head) for head in range(table_ref.shape[0])]
    running = []
    while waiting or running:
        if waiting and len(running) < 2:
            running.append(waiting.pop(0))
        for work in list(running):
            if next(work, running) is running:
                running.remove(work)


def call_kernel(inv_scale, half, full, pairs, coarse, tables, heads):
    rows, width = full[0].shape
    half_width = width // 2
    steps = heads // 2 // PER_STEP
    lanes = PER_STEP * LANES
    row_hot, key_hot, table, keep = tables

    def mine(h, half_ref):
        return (0, half_ref[0] * steps + h)

    def at(h, half_ref):
        return (0, h)

    def fixed(h, half_ref):
        return (0, 0)

    in_specs = (
        [pl.BlockSpec((rows, lanes), mine)] * 4
        + [pl.BlockSpec((2 * rows, lanes), at)] * 4
        + [pl.BlockSpec((x.shape[0], lanes), at) for x in coarse]
        + [
            pl.BlockSpec(row_hot.shape, fixed),
            pl.BlockSpec(key_hot.shape, fixed),
            pl.BlockSpec((PER_STEP, SLOT, LANES), lambda h, half_ref: (half_ref[0] * steps + h, 0, 0)),
            pl.BlockSpec(keep.shape, fixed),
        ]
    )
    out_rows = [4 * rows] * 2 + [2 * rows] * 2 + [x.shape[0] + SLOT for x in coarse]
    out_shape = [jax.ShapeDtypeStruct((r, half_width), BF16) for r in out_rows]
    out_specs = [pl.BlockSpec((r, lanes), at) for r in out_rows]
    return pl.pallas_call(
        functools.partial(attention_kernel, inv_scale),
        grid_spec=pltpu.PrefetchScalarGridSpec(
            num_scalar_prefetch=1, grid=(steps,), in_specs=in_specs, out_specs=out_specs
        ),
        out_shape=out_shape,
        compiler_params=pltpu.CompilerParams(
            dimension_semantics=("arbitrary",), vmem_limit_bytes=60 * 1024 * 1024
        ),
        cost_estimate=pl.CostEstimate(
            flops=12 * 2 * rows * 640 * half_width,
            bytes_accessed=10 * 1024 * 1024,
            transcendentals=heads * rows * 640,
        ),
    )(half, *full, *pairs, *coarse, row_hot, key_hot, table, keep)


def shards(queries, keys, values, grad_out, valid, scale_ids, scale_bias):
    q, k, v, g = queries[0], keys[0], values[0], grad_out[0]
    rows, width = q.shape
    half_width = width // 2
    heads, levels = scale_bias.shape[:2]
    tiles = lax.axis_size("tile")
    depth = tiles // 4
    images = lax.axis_size("batch")
    tile = lax.axis_index("tile")
    core = tile % 2
    inv_scale = 1.0 / math.sqrt(width // heads)
    half = core.reshape(1)

    def send(x, target):
        return lax.ppermute(x, "tile", [(i, target(i)) for i in range(tiles)])

    def to_core(x):
        return send(x, lambda i: i ^ 1)

    def to_side(x):
        return send(x, lambda i: i ^ 2)

    def to_corner(x):
        return send(x, lambda i: i ^ 3)

    def to_depth(x, distance):
        return send(x, lambda i: (i + 4 * distance) % tiles)

    edge = [(i, (i + 1 if i % 2 else i - 1) % tiles) for i in range(tiles)]
    jump = [(i, (i + 2 if i % 2 else i - 2) % tiles) for i in range(tiles)]

    def cut(x, which):
        return lax.dynamic_slice_in_dim(x, which * half_width, half_width, 1)

    def small(which):
        start, size = (0, which * half_width), (COARSE, half_width)
        return jnp.stack([lax.dynamic_slice(k, start, size), lax.dynamic_slice(v, start, size)])

    small_mine, small_other = small(core), small(1 - core)
    first = [small_mine, to_core(small_other), to_side(small_mine), to_corner(small_other)]
    kv_other = jnp.concatenate([cut(k, 1 - core), cut(v, 1 - core)], axis=0)
    kv_mine = jnp.concatenate([cut(k, core), cut(v, core)], axis=0)
    qg_other = jnp.concatenate([cut(q, 1 - core), cut(g, 1 - core)], axis=0)
    first[1], first[3], kv_other = lax.optimization_barrier((first[1], first[3], kv_other))
    kv_own_out = lax.ppermute(kv_other, "tile", edge)
    group = jnp.concatenate(first, axis=1).reshape(-1, half_width)
    kv_mine, qg_other, group = lax.optimization_barrier((kv_mine, qg_other, group))
    kv_par_out = lax.ppermute(kv_mine, "tile", jump)
    kv_par = to_core(kv_other)
    qg_par = to_core(qg_other)
    up_two = to_depth(group, -2)
    down_two = to_depth(group, 2)
    up_odd = to_depth(jnp.concatenate([group, up_two], axis=0), -1)
    down_odd = to_depth(jnp.concatenate([group, down_two], axis=0), 1)
    far = jnp.where(core == 0, up_two, down_two)
    far, kv_own_out = lax.optimization_barrier((far, kv_own_out))
    four = send(far, lambda i: (i + (8 if i % 2 else -8)) % tiles)
    coarse = [group, up_two, down_two, four, up_odd, down_odd]

    valid_grid = valid[0].reshape(tiles, rows)
    scale_grid = scale_ids.reshape(tiles, rows)
    level_grid = jnp.where(valid_grid > 0, scale_grid, levels)
    inner = jnp.arange(rows, dtype=jnp.int32)
    fine_grid = jnp.where(inner[None, :] >= COARSE, level_grid, levels)
    near_grid = jnp.pad(fine_grid, ((1, 1), (0, 0)), constant_values=levels)
    partner = tile ^ 1
    outward = 2 * core - 1

    def line(grid, index):
        return lax.dynamic_index_in_dim(grid, index, 0, keepdims=False)

    z_here = tile // 4
    spots = jnp.stack([((z_here + d) % depth) * 4 + (j ^ (tile % 4)) for d in OFFSETS for j in range(4)])
    pick = (spots[:, None] == jnp.arange(tiles, dtype=jnp.int32)[None, :]).astype(F32)
    coarse_level = jnp.dot(
        pick, level_grid[:, :COARSE].astype(F32), precision=lax.Precision.HIGHEST
    ).astype(jnp.int32)
    key_level = jnp.concatenate(
        [
            coarse_level.reshape(-1),
            line(near_grid, tile + 1),
            line(near_grid, partner + 1),
            line(near_grid, tile + 1 + outward),
            line(near_grid, partner + 1 - outward),
        ]
    )
    column = jnp.arange(LANES, dtype=jnp.int32)
    key_hot = (
        (key_level[:, None] == (column % SLOT)[None, :]) & (column < 3 * SLOT)[None, :]
    ).astype(BF16)
    row_level = jnp.concatenate([line(scale_grid, tile), line(scale_grid, partner)])
    row_hot = (row_level[:, None] == jnp.arange(SLOT, dtype=jnp.int32)[None, :]).astype(BF16)
    keep = jnp.concatenate([line(valid_grid, tile), line(valid_grid, partner)]).astype(F32)[:, None]

    level_ids = jnp.arange(levels, dtype=jnp.int32)
    scaled = jnp.where(
        (level_ids[None, :] <= level_ids[:, None])[None], scale_bias / inv_scale, MASKED
    )
    scaled = jnp.pad(
        scaled,
        ((0, 0), (0, SLOT - levels), (0, SLOT - levels)),
        constant_values=MASKED,
    )
    parts = []
    rest = scaled
    for _ in range(3):
        piece = lax.reduce_precision(rest, 8, 7)
        parts.append(piece)
        rest = rest - piece
    table = jnp.pad(
        jnp.concatenate(parts, axis=2), ((0, 0), (0, 0), (0, LANES - 3 * SLOT))
    ).astype(BF16)

    results = call_kernel(
        inv_scale,
        half,
        (q, k, v, g),
        (kv_par, qg_par, kv_own_out, kv_par_out),
        coarse,
        (row_hot, key_hot, table, keep),
        heads,
    )
    own, par, own_out, par_out = results[:4]
    here, up_two, down_two, four, up_odd, down_odd = results[4:10]

    def joined(mine, other_half):
        return jnp.where(
            core == 0,
            jnp.concatenate([mine, other_half], axis=-1),
            jnp.concatenate([other_half, mine], axis=-1),
        )

    every = images * tiles

    def flipped(x, mask):
        return lax.ppermute(x, ("batch", "tile"), [(i, i ^ mask) for i in range(every)])

    block, columns = here.shape

    def like(count, dtype):
        return jax.ShapeDtypeStruct((count, columns), dtype)

    def beside(pairs):
        return [p for p in pairs if p[0] // 4 == p[1] // 4], [p for p in pairs if p[0] // 4 != p[1] // 4]

    edge_y, edge_z = beside(edge)
    jump_y, jump_z = beside([(b, a) for a, b in jump])
    jump_y, jump_z = jump_y + [(i, i ^ 1) for i, _ in jump_z], jump_z + [(i, i ^ 1) for i, _ in jump_y]
    middle = (tile % 4 == 1) | (tile % 4 == 2)
    other_y = lax.ppermute(own_out, "tile", edge_y)
    mine_y = lax.ppermute(par_out, "tile", jump_y)
    other = to_core(par)
    up_odd = to_depth(up_odd, 1)
    down_odd = to_depth(down_odd, -1)
    four = send(four, lambda i: (i + (-8 if i % 2 else 8)) % tiles)
    up_odd, down_odd, four, own_out, par_out, other_y = lax.optimization_barrier(
        (up_odd, down_odd, four, own_out, par_out, other_y)
    )
    up_two, down_two = small_call(
        merge_kernel, half, (up_two, down_two, four, up_odd, down_odd), [like(block, BF16)] * 2
    )
    own_out, par_out, up_two, down_two = lax.optimization_barrier((own_out, par_out, up_two, down_two))
    other_z = lax.ppermute(own_out, "tile", edge_z)
    mine_z = lax.ppermute(par_out, "tile", jump_z)
    up_two = to_depth(up_two, 2)
    down_two = to_depth(down_two, -2)
    up_two, down_two, mine_y, other = lax.optimization_barrier((up_two, down_two, mine_y, other))
    kept, *quad = small_call(
        quad_kernel,
        None,
        (here, up_odd, down_odd, up_two, down_two),
        [like(2 * COARSE + SLOT, F32)] + [like(2 * COARSE + SLOT, BF16)] * 3,
    )
    quad = [to_core(quad[0]), to_side(quad[1]), to_corner(quad[2])]
    attended = joined(own[:rows], other[:rows])
    grad_q = joined(own[rows : 2 * rows], other[rows : 2 * rows])
    *quad, other_z = lax.optimization_barrier((*quad, other_z))
    fine_other = wide(other[2 * rows :]) + wide(other_y) + wide(other_z)
    coarse_rows, bias = small_call(
        finish_kernel,
        half,
        (kept, *quad),
        [
            jax.ShapeDtypeStruct((2 * COARSE, width), BF16),
            jax.ShapeDtypeStruct((2 * SLOT, LANES), F32),
        ],
    )
    bias = sum([flipped(bias, m * tiles) for m in (1, 2, 3)], bias)
    bias, mine_z, attended, grad_q = lax.optimization_barrier((bias, mine_z, attended, grad_q))
    bias = bias + flipped(bias, 4 * tiles)
    fine_mine = wide(own[2 * rows :]) + wide(jnp.where(middle, mine_y, mine_z))
    fine = joined(fine_mine, fine_other).astype(BF16)
    grad_bias = (
        bias.reshape(2, SLOT, heads // 2, SLOT)
        .transpose(0, 2, 1, 3)
        .reshape(heads, SLOT, SLOT)[:, :levels, :levels]
    )

    coarse_rows = coarse_rows.reshape(2, COARSE, width)
    fine = fine.reshape(2, rows, width)
    grads = jnp.concatenate([coarse_rows, fine[:, COARSE:]], axis=1)
    return (attended[None], grad_q[None], grads[0][None], grads[1][None], grad_bias)


def solution(mesh):
    block = P("batch", "tile", None)
    return jax.shard_map(
        shards,
        mesh=mesh,
        in_specs=(block, block, block, block, P("batch", None), P(), P()),
        out_specs=(block, block, block, block, P()),
        check_vma=False,
    )
```

```python
import functools
import math

import jax
import jax.numpy as jnp
from jax import lax
from jax.experimental import pallas as pl
from jax.experimental.pallas import tpu as pltpu
from jax.sharding import PartitionSpec as P

COARSE = 8
MASKED = -1e30
LANES = 128
SLOT = 16
PER_STEP = 2
BF16 = jnp.bfloat16
F32 = jnp.float32
OFFSETS = (0, 2, -2, 4, 1, 3, -1, -3)


def after(x, *done):
    return lax.optimization_barrier((x, *done))[0]


def mm(a, b, contract):
    return lax.dot_general(a, b, (contract, ((), ())), preferred_element_type=F32)


ROW_COL = ((1,), (0,))
ROW_ROW = ((1,), (1,))
COL_COL = ((0,), (0,))


def split_sum(x):
    lane = lax.broadcasted_iota(jnp.int32, x.shape, 1)
    high = x.astype(BF16).astype(F32)
    rest = x - high
    mid = rest.astype(BF16).astype(F32)
    low = rest - mid
    kept = jnp.where(lane < SLOT, high, jnp.where(lane < 2 * SLOT, mid, low))
    return jnp.where(lane < 3 * SLOT, kept, 0.0).astype(BF16)


def whole_sum(x):
    lane = lax.broadcasted_iota(jnp.int32, x.shape, 1)
    total = x + pltpu.roll(x, LANES - SLOT, 1) + pltpu.roll(x, LANES - 2 * SLOT, 1)
    return jnp.where(lane < SLOT, total, 0.0)


def resplit(x):
    total = whole_sum(x)
    return split_sum(total + pltpu.roll(total, SLOT, 1) + pltpu.roll(total, 2 * SLOT, 1))


def wide(x):
    return x.astype(F32)


def merge_kernel(half_ref, up_ref, down_ref, four_ref, up_odd_ref, down_odd_ref, up_out, down_out):
    block = up_ref.shape[0]
    across = wide(four_ref[...])
    upper = half_ref[0] == 0
    for ref, odd, far, out in (
        (up_ref, up_odd_ref, upper, up_out),
        (down_ref, down_odd_ref, jnp.logical_not(upper), down_out),
    ):
        total = wide(ref[...]) + wide(odd[block - SLOT :]) + jnp.where(far, across, 0.0)
        out[: block - SLOT] = total[: block - SLOT].astype(BF16)
        for h in range(0, total.shape[1], LANES):
            out[block - SLOT :, h : h + LANES] = resplit(total[block - SLOT :, h : h + LANES])


def quad_kernel(here_ref, up_ref, down_ref, up_two_ref, down_two_ref, keep_out, *outs):
    block = here_ref.shape[0]
    both = slice(0, block - SLOT), slice(2 * (block - SLOT), 2 * (block - SLOT) + SLOT)
    up = jnp.concatenate([wide(up_ref[rows]) for rows in both], axis=0)
    down = jnp.concatenate([wide(down_ref[rows]) for rows in both], axis=0)
    total = wide(here_ref[...]) + up + down
    total = total + wide(up_two_ref[...]) + wide(down_two_ref[...])
    part = (block - SLOT) // 2
    pieces = [
        jnp.concatenate(
            [total[j * COARSE : (j + 1) * COARSE], total[part + j * COARSE : part + (j + 1) * COARSE]],
            axis=0,
        )
        for j in range(4)
    ]
    tail = total[block - SLOT :]
    keep_out[: 2 * COARSE] = pieces[0]
    keep_out[2 * COARSE :] = tail
    bias = [resplit(tail[:, h : h + LANES]) for h in range(0, total.shape[1], LANES)]
    bias = jnp.concatenate(bias, axis=1)
    for piece, out in zip(pieces[1:], outs):
        out[: 2 * COARSE] = piece.astype(BF16)
        out[2 * COARSE :] = bias


def finish_kernel(half_ref, keep_ref, core_ref, side_ref, corner_ref, rows_out, bias_out):
    mine = keep_ref[...] + wide(side_ref[...])
    other = wide(core_ref[...]) + wide(corner_ref[...])
    first = half_ref[0] == 0
    low = jnp.where(first, mine, other)
    high = jnp.where(first, other, mine)
    rows_out[...] = jnp.concatenate([low[: 2 * COARSE], high[: 2 * COARSE]], axis=1).astype(BF16)
    for i, x in enumerate((low, high)):
        packed = jnp.zeros((SLOT, LANES), F32)
        for h in range(LANES // SLOT):
            one = whole_sum(x[2 * COARSE :, h * LANES : (h + 1) * LANES])
            packed = packed + (pltpu.roll(one, h * SLOT, 1) if h else one)
        bias_out[i * SLOT : (i + 1) * SLOT] = packed


def small_call(kernel, half, arrays, out_shape):
    smem = [pl.BlockSpec(memory_space=pltpu.SMEM)] if half is not None else []
    args = [half] if half is not None else []
    return pl.pallas_call(
        kernel,
        in_specs=smem + [pl.BlockSpec(memory_space=pltpu.VMEM)] * len(arrays),
        out_specs=[pl.BlockSpec(memory_space=pltpu.VMEM)] * len(out_shape),
        out_shape=out_shape,
        cost_estimate=pl.CostEstimate(flops=10**6, bytes_accessed=10**6, transcendentals=0),
    )(*args, *arrays)


def attention_kernel(inv_scale, half_ref, *refs):
    (q_ref, k_ref, v_ref, g_ref, kv_par, qg_par, kv_own_out, kv_par_out) = refs[:8]
    coarse_refs = refs[8:14]
    row_hot_ref, key_hot_ref, table_ref, keep_ref = refs[14:18]
    own_ref, par_ref, own_out_ref, par_out_ref = refs[18:22]
    coarse_out = refs[22:28]
    rows = q_ref.shape[0]
    part = coarse_refs[0].shape[0] // 2
    places = [(r, a) for r in range(len(coarse_refs)) for a in range(0, coarse_refs[r].shape[0], 2 * part)]
    total = part * len(places)
    keep = keep_ref[...] > 0.0
    row_hot = row_hot_ref[...]
    key_hot = key_hot_ref[...]

    def one_head(head):
        lanes = slice(head * LANES, (head + 1) * LANES)
        q = jnp.concatenate([q_ref[:, lanes], qg_par[:rows, lanes]], axis=0)
        g_all = jnp.concatenate([g_ref[:, lanes], qg_par[rows:, lanes]], axis=0)
        g = jnp.where(keep, g_all.astype(F32), 0.0).astype(BF16)
        k_main = jnp.concatenate([coarse_refs[r][a : a + part, lanes] for r, a in places] + [k_ref[:, lanes], kv_par[:rows, lanes]], axis=0)
        v_main = jnp.concatenate([coarse_refs[r][a + part : a + 2 * part, lanes] for r, a in places] + [v_ref[:, lanes], kv_par[rows:, lanes]], axis=0)
        main = k_main.shape[0]
        hot_main = key_hot[:main]
        hot_own = key_hot[main : main + rows]
        hot_par = key_hot[main + rows :]
        row_bias = mm(row_hot, table_ref[head], ROW_COL).astype(BF16)
        q_ext = jnp.concatenate([q, row_bias], axis=1)
        k_main_ext = jnp.concatenate([k_main, hot_main], axis=1)
        k_own_ext = jnp.concatenate([kv_own_out[:rows, lanes], hot_own], axis=1)
        k_par_ext = jnp.concatenate([kv_par_out[:rows, lanes], hot_par], axis=1)
        v_own = kv_own_out[rows:, lanes]
        v_par = kv_par_out[rows:, lanes]

        def stacked(a, own, par, contract):
            return jnp.concatenate([mm(a[:rows], own, contract), mm(a[rows:], par, contract)], axis=0)

        to_two = inv_scale * math.log2(math.e)
        s_main = mm(q_ext, k_main_ext, ROW_ROW)
        s_out = stacked(q_ext, k_own_ext, k_par_ext, ROW_ROW)
        gp_main = mm(g, v_main, ROW_ROW)
        gp_out = stacked(g, v_own, v_par, ROW_ROW)
        yield
        peak = jnp.maximum(
            jnp.max(s_main, axis=1, keepdims=True), jnp.max(s_out, axis=1, keepdims=True)
        )
        e_main = jnp.exp2((s_main - peak) * to_two)
        e_out = jnp.exp2((s_out - peak) * to_two)
        yield
        norm = 1.0 / (
            jnp.sum(e_main, axis=1, keepdims=True) + jnp.sum(e_out, axis=1, keepdims=True)
        )
        p_main = e_main * norm
        p_out = e_out * norm
        pb_main = p_main.astype(BF16)
        pb_out = p_out.astype(BF16)
        mixed = mm(pb_main, v_main, ROW_COL) + stacked(pb_out, v_own, v_par, ROW_COL)
        yield
        attended = jnp.where(keep, mixed, 0.0).astype(BF16)
        delta = jnp.sum(g.astype(F32) * mixed, axis=1, keepdims=True)
        d_main = p_main * (gp_main - delta)
        d_out = p_out * (gp_out - delta)
        db_main = d_main.astype(BF16)
        db_out = d_out.astype(BF16)
        dl_main = (d_main - db_main.astype(F32)).astype(BF16)
        dl_out = (d_out - db_out.astype(F32)).astype(BF16)
        yield
        q_terms = mm(db_main, k_main_ext, ROW_COL) + stacked(db_out, k_own_ext, k_par_ext, ROW_COL)
        grad_q = (q_terms[:, :LANES] * inv_scale).astype(BF16)
        by_level = q_terms[:, LANES:] + (
            mm(dl_main, hot_main, ROW_COL) + stacked(dl_out, hot_own, hot_par, ROW_COL)
        )
        bias = resplit(mm(row_hot, split_sum(by_level), COL_COL))
        yield
        gk_main = (mm(db_main, q, COL_COL) * inv_scale).astype(BF16)
        gv_main = mm(pb_main, g, COL_COL).astype(BF16)
        gk_own = (mm(db_out[:rows], q[:rows], COL_COL) * inv_scale).astype(BF16)
        gk_par = (mm(db_out[rows:], q[rows:], COL_COL) * inv_scale).astype(BF16)
        gv_own = mm(pb_out[:rows], g[:rows], COL_COL).astype(BF16)
        gv_par = mm(pb_out[rows:], g[rows:], COL_COL).astype(BF16)
        for place, ref in ((0, own_ref), (1, par_ref)):
            here = slice(place * rows, (place + 1) * rows)
            there = slice(total + place * rows, total + (place + 1) * rows)
            ref[0 * rows : 1 * rows, lanes] = attended[here]
            ref[1 * rows : 2 * rows, lanes] = grad_q[here]
            ref[2 * rows : 3 * rows, lanes] = gk_main[there]
            ref[3 * rows : 4 * rows, lanes] = gv_main[there]
        own_out_ref[:rows, lanes] = gk_own
        own_out_ref[rows:, lanes] = gv_own
        par_out_ref[:rows, lanes] = gk_par
        par_out_ref[rows:, lanes] = gv_par
        for ref in coarse_out:
            ref[ref.shape[0] - SLOT :, lanes] = bias
        for j, (r, a) in enumerate(places):
            coarse_out[r][a : a + part, lanes] = gk_main[j * part : (j + 1) * part]
            coarse_out[r][a + part : a + 2 * part, lanes] = gv_main[j * part : (j + 1) * part]

    waiting = [one_head(head) for head in range(table_ref.shape[0])]
    running = []
    while waiting or running:
        if waiting and len(running) < 2:
            running.append(waiting.pop(0))
        for work in list(running):
            if next(work, running) is running:
                running.remove(work)


def call_kernel(inv_scale, half, full, pairs, coarse, tables, heads):
    rows, width = full[0].shape
    half_width = width // 2
    steps = heads // 2 // PER_STEP
    lanes = PER_STEP * LANES
    row_hot, key_hot, table, keep = tables

    def mine(h, half_ref):
        return (0, half_ref[0] * steps + h)

    def at(h, half_ref):
        return (0, h)

    def fixed(h, half_ref):
        return (0, 0)

    in_specs = (
        [pl.BlockSpec((rows, lanes), mine)] * 4
        + [pl.BlockSpec((2 * rows, lanes), at)] * 4
        + [pl.BlockSpec((x.shape[0], lanes), at) for x in coarse]
        + [
            pl.BlockSpec(row_hot.shape, fixed),
            pl.BlockSpec(key_hot.shape, fixed),
            pl.BlockSpec((PER_STEP, SLOT, LANES), lambda h, half_ref: (half_ref[0] * steps + h, 0, 0)),
            pl.BlockSpec(keep.shape, fixed),
        ]
    )
    out_rows = [4 * rows] * 2 + [2 * rows] * 2 + [x.shape[0] + SLOT for x in coarse]
    out_shape = [jax.ShapeDtypeStruct((r, half_width), BF16) for r in out_rows]
    out_specs = [pl.BlockSpec((r, lanes), at) for r in out_rows]
    return pl.pallas_call(
        functools.partial(attention_kernel, inv_scale),
        grid_spec=pltpu.PrefetchScalarGridSpec(
            num_scalar_prefetch=1, grid=(steps,), in_specs=in_specs, out_specs=out_specs
        ),
        out_shape=out_shape,
        compiler_params=pltpu.CompilerParams(
            dimension_semantics=("arbitrary",), vmem_limit_bytes=60 * 1024 * 1024
        ),
        cost_estimate=pl.CostEstimate(
            flops=12 * 2 * rows * 640 * half_width,
            bytes_accessed=10 * 1024 * 1024,
            transcendentals=heads * rows * 640,
        ),
    )(half, *full, *pairs, *coarse, row_hot, key_hot, table, keep)


def shards(queries, keys, values, grad_out, valid, scale_ids, scale_bias):
    q, k, v, g = queries[0], keys[0], values[0], grad_out[0]
    rows, width = q.shape
    half_width = width // 2
    heads, levels = scale_bias.shape[:2]
    tiles = lax.axis_size("tile")
    depth = tiles // 4
    images = lax.axis_size("batch")
    tile = lax.axis_index("tile")
    core = tile % 2
    inv_scale = 1.0 / math.sqrt(width // heads)
    half = core.reshape(1)

    def send(x, target):
        return lax.ppermute(x, "tile", [(i, target(i)) for i in range(tiles)])

    def to_core(x):
        return send(x, lambda i: i ^ 1)

    def to_side(x):
        return send(x, lambda i: i ^ 2)

    def to_corner(x):
        return send(x, lambda i: i ^ 3)

    def to_depth(x, distance):
        return send(x, lambda i: (i + 4 * distance) % tiles)

    edge = [(i, (i + 1 if i % 2 else i - 1) % tiles) for i in range(tiles)]
    jump = [(i, (i + 2 if i % 2 else i - 2) % tiles) for i in range(tiles)]

    def cut(x, which):
        return lax.dynamic_slice_in_dim(x, which * half_width, half_width, 1)

    def small(which):
        start, size = (0, which * half_width), (COARSE, half_width)
        return jnp.stack([lax.dynamic_slice(k, start, size), lax.dynamic_slice(v, start, size)])

    small_mine, small_other = small(core), small(1 - core)
    first = [small_mine, to_core(small_other), to_side(small_mine), to_corner(small_other)]
    kv_other = jnp.concatenate([cut(k, 1 - core), cut(v, 1 - core)], axis=0)
    kv_mine = jnp.concatenate([cut(k, core), cut(v, core)], axis=0)
    qg_other = jnp.concatenate([cut(q, 1 - core), cut(g, 1 - core)], axis=0)
    first[1], first[3], kv_other = lax.optimization_barrier((first[1], first[3], kv_other))
    kv_own_out = lax.ppermute(kv_other, "tile", edge)
    group = jnp.concatenate(first, axis=1).reshape(-1, half_width)
    kv_mine, qg_other, group = lax.optimization_barrier((kv_mine, qg_other, group))
    kv_par_out = lax.ppermute(kv_mine, "tile", jump)
    kv_par = to_core(kv_other)
    qg_par = to_core(qg_other)
    up_two = to_depth(group, -2)
    down_two = to_depth(group, 2)
    up_odd = to_depth(jnp.concatenate([group, up_two], axis=0), -1)
    down_odd = to_depth(jnp.concatenate([group, down_two], axis=0), 1)
    far = jnp.where(core == 0, up_two, down_two)
    far, kv_own_out = lax.optimization_barrier((far, kv_own_out))
    four = send(far, lambda i: (i + (8 if i % 2 else -8)) % tiles)
    coarse = [group, up_two, down_two, four, up_odd, down_odd]

    valid_grid = valid[0].reshape(tiles, rows)
    scale_grid = scale_ids.reshape(tiles, rows)
    level_grid = jnp.where(valid_grid > 0, scale_grid, levels)
    inner = jnp.arange(rows, dtype=jnp.int32)
    fine_grid = jnp.where(inner[None, :] >= COARSE, level_grid, levels)
    near_grid = jnp.pad(fine_grid, ((1, 1), (0, 0)), constant_values=levels)
    partner = tile ^ 1
    outward = 2 * core - 1

    def line(grid, index):
        return lax.dynamic_index_in_dim(grid, index, 0, keepdims=False)

    z_here = tile // 4
    spots = jnp.stack([((z_here + d) % depth) * 4 + (j ^ (tile % 4)) for d in OFFSETS for j in range(4)])
    pick = (spots[:, None] == jnp.arange(tiles, dtype=jnp.int32)[None, :]).astype(F32)
    coarse_level = jnp.dot(
        pick, level_grid[:, :COARSE].astype(F32), precision=lax.Precision.HIGHEST
    ).astype(jnp.int32)
    key_level = jnp.concatenate(
        [
            coarse_level.reshape(-1),
            line(near_grid, tile + 1),
            line(near_grid, partner + 1),
            line(near_grid, tile + 1 + outward),
            line(near_grid, partner + 1 - outward),
        ]
    )
    column = jnp.arange(LANES, dtype=jnp.int32)
    key_hot = (
        (key_level[:, None] == (column % SLOT)[None, :]) & (column < 3 * SLOT)[None, :]
    ).astype(BF16)
    row_level = jnp.concatenate([line(scale_grid, tile), line(scale_grid, partner)])
    row_hot = (row_level[:, None] == jnp.arange(SLOT, dtype=jnp.int32)[None, :]).astype(BF16)
    keep = jnp.concatenate([line(valid_grid, tile), line(valid_grid, partner)]).astype(F32)[:, None]

    level_ids = jnp.arange(levels, dtype=jnp.int32)
    scaled = jnp.where(
        (level_ids[None, :] <= level_ids[:, None])[None], scale_bias / inv_scale, MASKED
    )
    scaled = jnp.pad(
        scaled,
        ((0, 0), (0, SLOT - levels), (0, SLOT - levels)),
        constant_values=MASKED,
    )
    parts = []
    rest = scaled
    for _ in range(3):
        piece = lax.reduce_precision(rest, 8, 7)
        parts.append(piece)
        rest = rest - piece
    table = jnp.pad(
        jnp.concatenate(parts, axis=2), ((0, 0), (0, 0), (0, LANES - 3 * SLOT))
    ).astype(BF16)

    results = call_kernel(
        inv_scale,
        half,
        (q, k, v, g),
        (kv_par, qg_par, kv_own_out, kv_par_out),
        coarse,
        (row_hot, key_hot, table, keep),
        heads,
    )
    own, par, own_out, par_out = results[:4]
    here, up_two, down_two, four, up_odd, down_odd = results[4:10]

    def joined(mine, other_half):
        return jnp.where(
            core == 0,
            jnp.concatenate([mine, other_half], axis=-1),
            jnp.concatenate([other_half, mine], axis=-1),
        )

    every = images * tiles

    def flipped(x, mask):
        return lax.ppermute(x, ("batch", "tile"), [(i, i ^ mask) for i in range(every)])

    block, columns = here.shape

    def like(count, dtype):
        return jax.ShapeDtypeStruct((count, columns), dtype)

    def beside(pairs):
        return [p for p in pairs if p[0] // 4 == p[1] // 4], [p for p in pairs if p[0] // 4 != p[1] // 4]

    edge_y, edge_z = beside(edge)
    edge_y = edge_y + [(i, i ^ 3) for i, _ in edge_z]
    jump_y, jump_z = beside([(b, a) for a, b in jump])
    jump_y, jump_z = jump_y + [(i, i ^ 1) for i, _ in jump_z], jump_z + [(i, i ^ 1) for i, _ in jump_y]
    middle = (tile % 4 == 1) | (tile % 4 == 2)
    other_y = lax.ppermute(own_out, "tile", edge_y)
    mine_y = lax.ppermute(par_out, "tile", jump_y)
    other = to_core(par)
    up_odd = to_depth(up_odd, 1)
    down_odd = to_depth(down_odd, -1)
    four = send(four, lambda i: (i + (-8 if i % 2 else 8)) % tiles)
    up_odd, down_odd, four, own_out, par_out, other_y = lax.optimization_barrier(
        (up_odd, down_odd, four, own_out, par_out, other_y)
    )
    up_two, down_two = small_call(
        merge_kernel, half, (up_two, down_two, four, up_odd, down_odd), [like(block, BF16)] * 2
    )
    own_out, par_out, up_two, down_two = lax.optimization_barrier((own_out, par_out, up_two, down_two))
    other_z = lax.ppermute(own_out, "tile", edge_z)
    mine_z = lax.ppermute(par_out, "tile", jump_z)
    up_two = to_depth(up_two, 2)
    down_two = to_depth(down_two, -2)
    up_two, down_two, mine_y, other = lax.optimization_barrier((up_two, down_two, mine_y, other))
    kept, *quad = small_call(
        quad_kernel,
        None,
        (here, up_odd, down_odd, up_two, down_two),
        [like(2 * COARSE + SLOT, F32)] + [like(2 * COARSE + SLOT, BF16)] * 3,
    )
    quad = [to_core(quad[0]), to_side(quad[1]), to_corner(quad[2])]
    attended = joined(own[:rows], other[:rows])
    grad_q = joined(own[rows : 2 * rows], other[rows : 2 * rows])
    *quad, other_z = lax.optimization_barrier((*quad, other_z))
    fine_other = wide(other[2 * rows :]) + wide(jnp.where(middle, other_y, other_z))
    coarse_rows, bias = small_call(
        finish_kernel,
        half,
        (kept, *quad),
        [
            jax.ShapeDtypeStruct((2 * COARSE, width), BF16),
            jax.ShapeDtypeStruct((2 * SLOT, LANES), F32),
        ],
    )
    bias = sum([flipped(bias, m * tiles) for m in (1, 2, 3)], bias)
    bias, mine_z, attended, grad_q = lax.optimization_barrier((bias, mine_z, attended, grad_q))
    bias = bias + flipped(bias, 4 * tiles)
    fine_mine = wide(own[2 * rows :]) + wide(jnp.where(middle, mine_y, mine_z))
    fine = joined(fine_mine, fine_other).astype(BF16)
    grad_bias = (
        bias.reshape(2, SLOT, heads // 2, SLOT)
        .transpose(0, 2, 1, 3)
        .reshape(heads, SLOT, SLOT)[:, :levels, :levels]
    )

    coarse_rows = coarse_rows.reshape(2, COARSE, width)
    fine = fine.reshape(2, rows, width)
    grads = jnp.concatenate([coarse_rows, fine[:, COARSE:]], axis=1)
    return (attended[None], grad_q[None], grads[0][None], grads[1][None], grad_bias)


def solution(mesh):
    block = P("batch", "tile", None)
    return jax.shard_map(
        shards,
        mesh=mesh,
        in_specs=(block, block, block, block, P("batch", None), P(), P()),
        out_specs=(block, block, block, block, P()),
        check_vma=False,
    )
```
